32 devices in a mesh: req: 4 (over x, core), mlp: 8 (over z, y).
Axes of the slice: x: 2, y: 2, z: 4, core: 2. Of those that a mesh axis runs over, the one named last changes fastest.
Arguments:
- residual_in: bfloat16 [4096, 1792], P(('req', 'mlp')), may hold values from -6 to 6
- query_in: bfloat16 [4096, 256], P(('req', 'mlp')), may hold values from -4 to 4
- key_in: bfloat16 [4096, 256], P(('req', 'mlp')), may hold values from -4 to 4
- values_in: bfloat16 [4096, 1792], P(('req', 'mlp')), may hold values from -6 to 6
- conv_weight: float32 [3, 1792], replicated, may hold values from -0.8 to 0.8
- prefix_state: float32 [4, 16, 273, 112], P('req', 'mlp'), may hold values from -896 to 896
- prefix_norm: float32 [4, 16, 273], P('req', 'mlp'), as said below
- prefix_owner: int32 [4], replicated, may hold values from 0 to 3, each once
- lengths: int32 [4, 4], P('req'), may hold values from 1 to 512, 1024 in all within a row
- old_flags: int32 [4, 4], P('req'), may hold values 0 or 1
- out_weight: bfloat16 [1792, 1792], replicated, may hold values from -0.125 to 0.125
- mlp_gain: float32 [1792], replicated, may hold values from 0.5 to 1.5
- gate_weight: bfloat16 [1792, 4864], P(None, 'mlp'), may hold values from -0.125 to 0.125
- up_weight: bfloat16 [1792, 4864], P(None, 'mlp'), may hold values from -0.125 to 0.125
- down_weight: bfloat16 [4864, 1792], P('mlp'), may hold values from -0.078125 to 0.078125
- next_gain: float32 [1792], replicated, may hold values from 0.5 to 1.5
- qkv_weight: bfloat16 [1792, 2304], replicated, may hold values from -0.125 to 0.125
Outputs:
- hidden_out: bfloat16 [4096, 1792], P(('req', 'mlp'))
- next_qkv: bfloat16 [4096, 2304], P(('req', 'mlp'))
The draws below stay inside these ranges and needn't reach their ends.
Inputs may be any that keep to these rules, and one draw needn't show every extreme that they name: `prefix_owner`: each slot holds exactly one group's cached state. `lengths`: a group's requests follow one another in order and fill its 1024 tokens; the longest of a group has exactly half of 1024. `prefix_norm`: a head's cached normalizer is a sum of feature maps of earlier keys.
All inputs are finite; a program needn't handle non-finite values. No bound on the sum of `old_flags` on one device may be relied on, other than what follows from the above.
Results may differ from the reference program's by a relative error of at most 0.024.
Values may be sent and summed in bfloat16 or wider, within the bound.
No kernel may reach another device: no remote copies, remote signals or barrier semaphores. Data moves between devices by JAX's collectives and lax.ppermute only.
A program may use at most 192 MiB of HBM per device.

```python
import math
import jax
import jax.numpy as jnp
import numpy as np
from jax import lax

D = 1792
H = 16
FD = 16
FF = 4864
CONV = 3
RQ = 4
HD = 112
FEAT = 273
QKV = 2304
SEQ = 1024
TOKENS = 4096
N_REQ = 4
N_MLP = 8


def draw_prefix_norm(key, part):
    key_points = jax.random.fold_in(key, 11)
    key_weights = jax.random.fold_in(key, 12)
    shape = (N_REQ, H, 32, FD)
    points = jax.random.normal(key_points, shape, jnp.float32)
    weights = jnp.exp(jax.random.uniform(key_weights, (N_REQ, H, 32), jnp.float32, math.log(4.0), math.log(64.0)))
    squares = (points[..., :, None] * points[..., None, :]).reshape(N_REQ, H, 32, FD * FD)
    constant = jnp.ones((N_REQ, H, 32, 1), jnp.float32)
    features = jnp.concatenate([constant, points * FD ** (-0.25), squares / (math.sqrt(2.0) * math.sqrt(FD))], axis=-1)
    return jnp.sum(weights[..., None] * features, axis=2)


def set_ends(result, key, low, largest):
    dims = result.shape
    spot = [jax.random.randint(jax.random.fold_in(key, axis), (), 0, dims[axis]) for axis in range(len(dims))]
    result = result.at[tuple(spot)].set(low)
    longest = dims.index(max(dims))
    spot[longest] = (spot[longest] + 1) % dims[longest]
    return result.at[tuple(spot)].set(largest)


def level_of(stream_key, dims, shards, least, top_value):
    level, own = 1.0, jax.random.fold_in(stream_key, 6)
    for dim, blocks in shards:
        steps = jnp.exp(jax.random.uniform(jax.random.fold_in(own, dim), (blocks,), jnp.float32, least / len(shards), top_value / len(shards)))
        level = level * jnp.repeat(steps, dims[dim] // blocks).reshape([-1 if axis == dim else 1 for axis in range(len(dims))])
    return level


def profile(count, total, bound, skew):
    loads = [(1 << 20) // math.isqrt(standing ** skew) + 1 for standing in range(2, count + 1)]
    rest, given = total - bound - (count - 1), [1] * (count - 1)
    while rest > 0:
        candidates = [i for i in range(count - 1) if given[i] < bound]
        pool, left = sum([loads[i] for i in candidates]), rest
        for i in candidates:
            more = min(bound - given[i], max(1, left * loads[i] // pool), rest)
            given[i] = given[i] + more
            rest = rest - more
    return np.array([bound] + given)


def ragged(key, number_of, total, bound, lean):
    if number_of == 2:
        one = jax.random.randint(key, (), max(1, total - bound), min(bound, total - 1) + 1)
        return jnp.stack([one, total - one])
    tallies = jnp.asarray(profile(number_of, total, bound, lean), jnp.int32)
    twos = (number_of - 1) // 2
    source_of, sink = tallies[1:1 + 2 * twos:2], tallies[2:2 + 2 * twos:2]
    room = jnp.minimum(source_of - 1, bound - sink)
    shifted = jax.random.randint(jax.random.fold_in(key, 1), (twos,), 0, 1 << 20) % (room + 1)
    tallies = tallies.at[1:1 + 2 * twos:2].set(source_of - shifted).at[2:2 + 2 * twos:2].set(sink + shifted)
    return tallies[jax.random.permutation(jax.random.fold_in(key, 2), number_of)]


def scatter_about(rng, shape, scale, bound, split=(), held_as=jnp.bfloat16):
    level = level_of(rng, shape, split, -0.22, 0.18) if split else 1.0
    values = jax.random.normal(rng, shape, jnp.float32) * scale * level
    return jnp.minimum(jnp.maximum(values, -bound), bound).astype(held_as)


def setup_inputs(seed: int = 0) -> dict:
    splits = jax.random.split(jax.random.key(seed), 18)
    residual_in = scatter_about(splits[0], (TOKENS, D), 1.0, 6.0, ((0, 32),))
    query_in = scatter_about(splits[1], (TOKENS, H * FD), 1.0, 4.0, ((0, 32),))
    key_in = scatter_about(splits[2], (TOKENS, H * FD), 1.0, 4.0, ((0, 32),))
    values_in = scatter_about(splits[3], (TOKENS, D), 1.0, 6.0, ((0, 32),))
    conv_weight = jnp.clip(jax.random.uniform(splits[4], (CONV, D), jnp.float32, -0.8, 0.8), -0.8, 0.8)
    prefix_state = scatter_about(splits[5], (N_REQ, H, FEAT, HD), 140.0, 896.0, ((0, 4), (1, 8)), jnp.float32)
    prefix_norm = draw_prefix_norm(jax.random.fold_in(splits[17], 71), 0)
    prefix_owner = jax.random.permutation(splits[7], N_REQ).astype(jnp.int32)
    lengths = jax.vmap(lambda own: ragged(own, RQ, SEQ, SEQ // 2, 2))(jax.random.split(splits[8], N_REQ)).reshape((N_REQ, RQ)).astype(jnp.int32)
    old_flags = set_ends((jax.random.randint(splits[9], (N_REQ, RQ), 0, 2) < 1).astype(jnp.int32), jax.random.fold_in(splits[9], 1), 0, 1)
    out_weight = scatter_about(splits[10], (D, D), D ** -0.5, 0.125)
    mlp_gain = jnp.clip(1.0 + 0.1 * jax.random.normal(splits[11], (D,), jnp.float32), 0.5, 1.5)
    gate_weight = scatter_about(splits[12], (D, FF), D ** -0.5, 0.125, ((1, 8),))
    up_weight = scatter_about(splits[13], (D, FF), D ** -0.5, 0.125, ((1, 8),))
    down_weight = scatter_about(splits[14], (FF, D), FF ** -0.5, 0.078125, ((0, 8),))
    next_gain = jnp.clip(1.0 + 0.1 * jax.random.normal(splits[15], (D,), jnp.float32), 0.5, 1.5)
    qkv_weight = scatter_about(splits[16], (D, QKV), D ** -0.5, 0.125)
    return {"residual_in": residual_in, "query_in": query_in, "key_in": key_in, "values_in": values_in, "conv_weight": conv_weight, "prefix_state": prefix_state, "prefix_norm": prefix_norm, "prefix_owner": prefix_owner, "lengths": lengths, "old_flags": old_flags, "out_weight": out_weight, "mlp_gain": mlp_gain, "gate_weight": gate_weight, "up_weight": up_weight, "down_weight": down_weight, "next_gain": next_gain, "qkv_weight": qkv_weight}


EPSILON = 1e-05
HIGHEST = lax.Precision.HIGHEST

def feature_map(entries):
    feat_dim = entries.shape[-1]
    leading = entries.shape[:-1]
    squares = (entries[..., :, None] * entries[..., None, :]).reshape(leading + (feat_dim * feat_dim,))
    constant = jnp.ones(leading + (1,), jnp.float32)
    return jnp.concatenate([constant, entries * feat_dim ** (-0.25), squares / (math.sqrt(2.0) * math.sqrt(feat_dim))], axis=-1)

def request_of(lengths, positions):
    boundary = jnp.cumsum(lengths).astype(jnp.int32)[:-1]
    which = lax.optimization_barrier(jnp.sum((positions[:, None] >= boundary[None, :]).astype(jnp.int32), axis=1)).astype(jnp.int32)
    return jnp.where(positions < 0, jnp.int32(-1), which).astype(jnp.int32)

def convolve(entries, weights, requests, earlier_rows, earlier_requests):
    tap_count = weights.shape[0]
    row_count = entries.shape[0]
    extended = jnp.concatenate([earlier_rows, entries], axis=0).astype(jnp.float32)
    request_rows = jnp.concatenate([earlier_requests, requests], axis=0)
    summed = jnp.zeros(entries.shape, jnp.float32)
    for shift_by in range(tap_count):
        first_row = tap_count - 1 - shift_by
        earlier = extended[first_row:first_row + row_count]
        matching = (request_rows[first_row:first_row + row_count] == requests)[:, None]
        summed = summed + weights[shift_by][None, :] * jnp.where(matching, earlier, 0.0)
    return summed.astype(jnp.bfloat16)

def block_output(feat_query, feat_key, entries, requests, before, token_flags, carry_state, carry_norm, prefix_state, prefix_norm):
    row_count = requests.shape[0]
    scores = jnp.einsum('bhf,chf->hbc', feat_query.astype(jnp.float32), feat_key.astype(jnp.float32), precision=HIGHEST)
    row_index = jnp.arange(row_count)
    visible = (row_index[:, None] >= row_index[None, :]) & (requests[:, None] == requests[None, :])
    scores = jnp.where(visible[None], scores, 0.0)
    normalizer = jnp.transpose(lax.optimization_barrier(jnp.sum(scores, axis=2)))
    numerator = jnp.einsum('hbc,che->bhe', scores.astype(jnp.bfloat16).astype(jnp.float32), entries.astype(jnp.float32), precision=HIGHEST)
    continues = (requests == before).astype(jnp.float32)
    query_wide = feat_query.astype(jnp.float32)
    numerator = numerator + token_flags[:, None, None] * jnp.einsum('bhf,hfe->bhe', query_wide, prefix_state, precision=HIGHEST)
    numerator = numerator + continues[:, None, None] * jnp.einsum('bhf,hfe->bhe', query_wide, carry_state, precision=HIGHEST)
    normalizer = normalizer + token_flags[:, None] * jnp.einsum('bhf,hf->bh', query_wide, prefix_norm, precision=HIGHEST)
    normalizer = normalizer + continues[:, None] * jnp.einsum('bhf,hf->bh', query_wide, carry_norm, precision=HIGHEST)
    return (numerator / normalizer[:, :, None]).astype(jnp.bfloat16)

def block_state(feat_key, entries, requests, before):
    in_last = (requests == requests[-1]).astype(jnp.float32)
    keys_last = feat_key.astype(jnp.float32) * in_last[:, None, None]
    state = jnp.einsum('bhf,bhe->hfe', keys_last, entries.astype(jnp.float32), precision=HIGHEST)
    norm_sum = lax.optimization_barrier(jnp.sum(keys_last, axis=0))
    started = (requests[-1] != before).astype(jnp.float32)
    return (state, norm_sum, started)

def run_blocks(query, key_rows, conv_values, requests, token_flags, prefix_state, prefix_norm, block_rows):
    total_rows, head_count, feat_dim = query.shape
    head_width = conv_values.shape[2]
    feat_total = 1 + feat_dim + feat_dim * feat_dim
    steps_count = total_rows // block_rows

    def advance(carried, inputs):
        carry_state, carry_norm, before = carried
        query_block, key_block, value_block, request_block, flag_block = inputs
        feat_query = feature_map(query_block.astype(jnp.float32)).astype(jnp.bfloat16)
        feat_key = feature_map(key_block.astype(jnp.float32)).astype(jnp.bfloat16)
        output = block_output(feat_query, feat_key, value_block, request_block, before, flag_block, carry_state, carry_norm, prefix_state, prefix_norm)
        state, norm_sum, started = block_state(feat_key, value_block, request_block, before)
        keeping = 1.0 - started
        return ((state + keeping * carry_state, norm_sum + keeping * carry_norm, request_block[-1]), output)
    initial = (jnp.zeros((head_count, feat_total, head_width), jnp.float32), jnp.zeros((head_count, feat_total), jnp.float32), jnp.array(-1, dtype=jnp.int32))
    inputs = (query.reshape(steps_count, block_rows, head_count, feat_dim), key_rows.reshape(steps_count, block_rows, head_count, feat_dim), conv_values.reshape(steps_count, block_rows, head_count, head_width), requests.reshape(steps_count, block_rows), token_flags.reshape(steps_count, block_rows))
    _, outputs = lax.scan(advance, initial, inputs)
    return outputs.reshape(total_rows, head_count, head_width)

def flag_lookup(requests, request_ids, flag_row):
    matches = requests[:, None] == request_ids[None, :]
    return lax.optimization_barrier(jnp.sum(jnp.where(matches, flag_row[None, :], 0.0), axis=1))

def rms_scale(entries, gain):
    return entries * lax.rsqrt(lax.optimization_barrier(jnp.mean(entries * entries, axis=-1, keepdims=True)) + EPSILON) * gain

def reference(residual_in, query_in, key_in, values_in, conv_weight, prefix_state, prefix_norm, prefix_owner, lengths, old_flags, out_weight, mlp_gain, gate_weight, up_weight, down_weight, next_gain, qkv_weight):
    shard_width = FF // N_MLP

    def one_group(group_id):
        first_row = (group_id * SEQ).astype(jnp.int32)
        residual = lax.dynamic_slice_in_dim(residual_in, first_row, SEQ, 0)
        query = lax.dynamic_slice_in_dim(query_in, first_row, SEQ, 0).reshape(SEQ, H, FD)
        key_rows = lax.dynamic_slice_in_dim(key_in, first_row, SEQ, 0).reshape(SEQ, H, FD)
        value_rows = lax.dynamic_slice_in_dim(values_in, first_row, SEQ, 0)
        positions = jnp.arange(SEQ, dtype=jnp.int32)
        requests = request_of(lengths[group_id], positions)
        conv_values = convolve(value_rows, conv_weight, requests, jnp.zeros((CONV - 1, D), jnp.bfloat16), jnp.full((CONV - 1,), -1, jnp.int32))
        token_flags = flag_lookup(requests, jnp.arange(RQ, dtype=jnp.int32), old_flags[group_id].astype(jnp.float32))
        owner_slot = prefix_owner[group_id]
        attended = run_blocks(query, key_rows, conv_values.reshape(SEQ, H, HD), requests, token_flags, prefix_state[owner_slot], prefix_norm[owner_slot], min(SEQ, 512))
        projected = jnp.dot(attended.reshape(SEQ, D), out_weight, preferred_element_type=jnp.float32)
        first_sum = (residual.astype(jnp.float32) + projected).astype(jnp.bfloat16)
        normed = rms_scale(first_sum.astype(jnp.float32), mlp_gain).astype(jnp.bfloat16)
        gate_rows = jnp.dot(normed, gate_weight, preferred_element_type=jnp.float32)
        up_rows = jnp.dot(normed, up_weight, preferred_element_type=jnp.float32)
        hidden = (jax.nn.silu(gate_rows) * up_rows).astype(jnp.bfloat16)

        def add_shard(summed, shard_id):
            offset = (shard_id * shard_width).astype(jnp.int32)
            partial_sum = jnp.dot(lax.dynamic_slice_in_dim(hidden, offset, shard_width, 1), lax.dynamic_slice_in_dim(down_weight, offset, shard_width, 0), preferred_element_type=jnp.float32)
            rounded = lax.optimization_barrier(partial_sum.astype(jnp.bfloat16)).astype(jnp.float32)
            return (summed + rounded, None)
        mlp_output, _ = lax.scan(add_shard, jnp.zeros((SEQ, D), jnp.float32), jnp.arange(N_MLP, dtype=jnp.int32))
        second_sum = (first_sum.astype(jnp.float32) + mlp_output).astype(jnp.bfloat16)
        normed_next = rms_scale(second_sum.astype(jnp.float32), next_gain).astype(jnp.bfloat16)
        projections = jnp.dot(normed_next, qkv_weight, preferred_element_type=jnp.float32).astype(jnp.bfloat16)
        return (second_sum, projections)
    second_sum, projections = lax.map(one_group, jnp.arange(N_REQ, dtype=jnp.int32))
    return (second_sum.reshape(TOKENS, D), projections.reshape(TOKENS, QKV))
```

```python
import functools
import math

import jax
import jax.numpy as jnp
from jax import lax
from jax.experimental import pallas as pl
from jax.experimental.pallas import tpu as pltpu
from jax.sharding import PartitionSpec as P

EPSILON = 1e-05
DEPTH = 4
MIB = 1 << 20
ACROSS = (((0,), (0,)), ((), ()))
PLAIN = (((1,), (0,)), ((), ()))
F32 = jnp.float32
BF16 = jnp.bfloat16
VMEM = pltpu.VMEM


def vmem():
    return pl.BlockSpec(memory_space=VMEM)


def dot(a, b, dims=PLAIN):
    return lax.dot_general(a, b, dims, preferred_element_type=F32)


def pack_kernel(q_ref, k_ref, v_ref, out_ref):
    count = out_ref.shape[0]
    at = 0
    for ref in (q_ref, k_ref, v_ref):
        turned = ref[...].T
        part = turned.shape[0] // count
        for m in range(count):
            out_ref[m, at : at + part, :] = turned[m * part : (m + 1) * part, :]
        at += part


def pack(q, k, v, count):
    rows = (q.shape[1] + k.shape[1] + v.shape[1]) // count
    return pl.pallas_call(
        pack_kernel,
        out_shape=jax.ShapeDtypeStruct((count, rows, q.shape[0]), BF16),
        in_specs=[vmem()] * 3,
        out_specs=vmem(),
        compiler_params=pltpu.CompilerParams(vmem_limit_bytes=24 * MIB),
        name="pack_heads",
    )(q, k, v)


def attention_kernel(heads, fd, hd, meta_ref, x_ref, conv_ref, state_ref, out_ref, turned, vconv, feats):
    blocks, rows, local = x_ref.shape
    tokens = blocks * local
    requests = meta_ref.shape[1]
    values_at = 2 * heads * fd
    tile = 256 if tokens % 256 == 0 else local
    for m in range(blocks):
        turned[:, m * local : (m + 1) * local] = x_ref[m]

    position = lax.broadcasted_iota(jnp.int32, (1, tokens), 1)
    start = jnp.zeros((1, tokens), jnp.int32)
    flag = jnp.zeros((1, tokens), F32) + meta_ref[1, 0].astype(F32)
    boundary = jnp.int32(0)
    for r in range(1, requests):
        boundary = boundary + meta_ref[0, r - 1]
        reached = position >= boundary
        start = jnp.where(reached, boundary, start)
        flag = jnp.where(reached, meta_ref[1, r].astype(F32), flag)

    values = turned[values_at:, :].astype(F32)
    total = conv_ref[:, 0:1] * values
    for tap in range(1, conv_ref.shape[1]):
        earlier = pltpu.roll(values, tap, 1)
        total = total + conv_ref[:, tap : tap + 1] * jnp.where(position - tap >= start, earlier, 0.0)
    vconv[...] = total.astype(BF16)

    for h in range(heads):
        query = turned[h * fd : (h + 1) * fd, :]
        wide = query.astype(F32)
        scaled = wide * (1.0 / math.sqrt(2.0 * fd))
        for a in range(fd):
            feats[a * fd : (a + 1) * fd, :] = (wide[a : a + 1, :] * scaled).astype(BF16)
        feats[fd * fd : fd * fd + fd, :] = (wide * fd ** (-0.25)).astype(BF16)
        ones = lax.broadcasted_iota(jnp.int32, (16, tokens), 0) == 0
        feats[fd * fd + fd :, :] = ones.astype(F32).astype(BF16)
        key = turned[(heads + h) * fd : (heads + h + 1) * fd, :]
        for first in range(0, tokens, tile):
            last = first + tile
            old = dot(state_ref[h], feats[:, first:last], ACROSS)
            score = dot(key[:, :last], query[:, first:last], ACROSS) * (fd**-0.5) + 1.0
            score = score * score * 0.5 + 0.5
            key_at = lax.broadcasted_iota(jnp.int32, (last, tile), 0)
            visible = (key_at >= start[:, first:last]) & (key_at <= position[:, first:last])
            score = jnp.where(visible, score, 0.0)
            den = jnp.sum(score, axis=0, keepdims=True) + flag[:, first:last] * old[hd : hd + 1, :]
            num = dot(vconv[h * hd : (h + 1) * hd, :last], score.astype(BF16))
            num = num + flag[:, first:last] * old[:hd, :]
            result = (num / den).astype(BF16)
            for at in range(first, last, local):
                out_ref[at // local, h * hd : (h + 1) * hd, :] = result[:, at - first : at - first + local]


def attention(meta, x, conv, state, heads, fd, hd):
    blocks, rows, local = x.shape
    tokens = blocks * local
    return pl.pallas_call(
        functools.partial(attention_kernel, heads, fd, hd),
        out_shape=jax.ShapeDtypeStruct((blocks, heads * hd, local), BF16),
        in_specs=[pl.BlockSpec(memory_space=pltpu.SMEM)] + [vmem()] * 3,
        out_specs=vmem(),
        scratch_shapes=[
            VMEM((rows, tokens), BF16),
            VMEM((heads * hd, tokens), BF16),
            VMEM((state.shape[1], tokens), BF16),
        ],
        compiler_params=pltpu.CompilerParams(vmem_limit_bytes=40 * MIB),
        name="attention",
    )(meta, x, conv, state)


def rms(rows, gain):
    return rows * lax.rsqrt(jnp.mean(rows * rows, axis=-1, keepdims=True) + EPSILON) * gain


def project_kernel(tile, att_ref, w_ref, res_ref, gain_ref, sum_ref, normed_ref, rows):
    step = pl.program_id(0)

    @pl.when(step == 0)
    def _():
        rows[...] = att_ref[...].T

    at = pl.ds(pl.multiple_of(step * tile, tile), tile)
    projected = dot(rows[...], w_ref[...])
    sum_ref[:, at] = (res_ref[:, at].astype(F32) + projected).astype(BF16)

    @pl.when(step == pl.num_programs(0) - 1)
    def _():
        normed_ref[...] = rms(sum_ref[...].astype(F32), gain_ref[...]).astype(BF16)


def project(att, w, residual, gain):
    depth, rows = att.shape
    width = w.shape[1]
    tile = 256
    whole = lambda shape: pl.BlockSpec(shape, lambda i: (0, 0))
    return pl.pallas_call(
        functools.partial(project_kernel, tile),
        grid=(width // tile,),
        out_shape=[jax.ShapeDtypeStruct((rows, width), BF16)] * 2,
        in_specs=[
            whole((depth, rows)),
            pl.BlockSpec((depth, tile), lambda i: (0, i)),
            whole((rows, width)),
            whole((1, width)),
        ],
        out_specs=[whole((rows, width))] * 2,
        scratch_shapes=[VMEM((rows, depth), BF16)],
        compiler_params=pltpu.CompilerParams(vmem_limit_bytes=24 * MIB),
        name="out_projection",
    )(att, w, residual, gain)


def mlp_kernel(inputs, sides, flips, *refs):
    it = iter(refs)
    take = lambda n: [next(it) for _ in range(n)]
    xs = take(inputs)
    own = take(3)
    pieces = [[take(2) for _ in flips] for _ in range(sides)]
    outs = take(inputs)
    gates, ups, downs, sems = take(4)
    me = lax.axis_index("req")
    copies = [
        pltpu.make_async_copy(own[0], gates.at[0], sems.at[0]),
        pltpu.make_async_copy(own[1], ups.at[0], sems.at[1]),
        pltpu.make_async_copy(own[2], downs.at[0, pl.ds(0, own[2].shape[0])], sems.at[2]),
    ]
    index = 3
    for side in range(sides):
        for flip, (gate_up, down) in zip(flips, pieces[side]):
            slot = me ^ flip
            deep, tall = gate_up.shape[1], down.shape[0]
            at = pl.ds(pl.multiple_of(slot * deep, 16), deep)
            low = pl.ds(pl.multiple_of(slot * tall, 16), tall)
            copies.append(pltpu.make_async_copy(gate_up.at[0], gates.at[1 + side, at], sems.at[index]))
            copies.append(pltpu.make_async_copy(gate_up.at[1], ups.at[1 + side, at], sems.at[index + 1]))
            copies.append(pltpu.make_async_copy(down, downs.at[1 + side, low], sems.at[index + 2]))
            index += 3
    for copy in copies:
        copy.start()
    x = xs[0][...] if inputs == 1 else jnp.concatenate([ref[...] for ref in xs], axis=0)
    hidden_units = own[0].shape[1]
    per_side = 3 * len(flips)
    total = None
    for side in range(1 + sides):
        for copy in copies[:3] if side == 0 else copies[3 + (side - 1) * per_side : 3 + side * per_side]:
            copy.wait()
        gate = dot(x, gates[side])
        up = dot(x, ups[side])
        hidden = (gate * jax.nn.sigmoid(gate) * up).astype(BF16)
        part = dot(hidden, downs[side, :hidden_units, :])
        total = part if total is None else total + part
    local = xs[0].shape[0]
    for i, out in enumerate(outs):
        out[...] = total[i * local : (i + 1) * local].astype(BF16)


def mlp(xs, own, pieces, flips):
    deep, units = own[0].shape
    sides = len(pieces)
    tall = pieces[0][0][1].shape[0] * len(flips) if sides else units
    flat = [ref for side in pieces for piece in side for ref in piece]
    rows = xs[0].shape[0]
    weight_bytes = 2 * (1 + sides) * 3 * deep * units
    return pl.pallas_call(
        functools.partial(mlp_kernel, len(xs), sides, flips),
        out_shape=[jax.ShapeDtypeStruct((rows, deep), BF16)] * len(xs),
        in_specs=[vmem()] * len(xs) + [pl.BlockSpec(memory_space=pl.ANY)] * (3 + len(flat)),
        out_specs=[vmem()] * len(xs),
        scratch_shapes=[
            VMEM((1 + sides, deep, units), BF16),
            VMEM((1 + sides, deep, units), BF16),
            VMEM((1 + sides, max(tall, units), deep), BF16),
            pltpu.SemaphoreType.DMA((3 + 3 * sides * len(flips),)),
        ],
        compiler_params=pltpu.CompilerParams(vmem_limit_bytes=40 * MIB),
        cost_estimate=pl.CostEstimate(
            flops=6 * len(xs) * rows * (1 + sides) * deep * units,
            bytes_accessed=weight_bytes,
            transcendentals=0,
        ),
        name="feed_forward",
    )(*xs, *own, *flat)


def next_kernel(tile, first_ref, own_ref, left_ref, right_ref, gain_ref, w_ref, sum_ref, out_ref, normed):
    step = pl.program_id(0)

    @pl.when(step == 0)
    def _():
        extra = own_ref[...].astype(F32) + left_ref[...].astype(F32) + right_ref[...].astype(F32)
        second = (first_ref[...].astype(F32) + extra).astype(BF16)
        sum_ref[...] = second
        normed[...] = rms(second.astype(F32), gain_ref[...]).astype(BF16)

    out_ref[...] = dot(normed[...], w_ref[...]).astype(BF16)


def next_projection(first, own, left, right, gain, w):
    rows, deep = first.shape
    width = w.shape[1]
    tile = 256
    whole = lambda shape: pl.BlockSpec(shape, lambda i: (0, 0))
    return pl.pallas_call(
        functools.partial(next_kernel, tile),
        grid=(width // tile,),
        out_shape=[
            jax.ShapeDtypeStruct((rows, deep), BF16),
            jax.ShapeDtypeStruct((rows, width), BF16),
        ],
        in_specs=[whole((rows, deep))] * 4
        + [whole((1, deep)), pl.BlockSpec((deep, tile), lambda i: (0, i))],
        out_specs=[whole((rows, deep)), pl.BlockSpec((rows, tile), lambda i: (0, i))],
        scratch_shapes=[VMEM((rows, deep), BF16)],
        compiler_params=pltpu.CompilerParams(vmem_limit_bytes=24 * MIB),
        name="next_projection",
    )(first, own, left, right, gain, w)


def side_weights(gate, up, down, width):
    sharers = lax.axis_size("req")
    me = lax.axis_index("req")
    depth = lax.axis_size("mlp") // width
    deep = gate.shape[0] // sharers
    tall = -(-down.shape[0] // (16 * sharers)) * 16
    padded = jnp.pad(down, ((0, tall * sharers - down.shape[0]), (0, 0)))
    mine = (
        jnp.stack([lax.dynamic_slice_in_dim(w, me * deep, deep, 0) for w in (gate, up)]),
        lax.dynamic_slice_in_dim(padded, me * tall, tall, 0),
    )
    sides, flips = [], []
    for turn in range(1, width):
        route = [
            (z * width + y, z * width + (y + turn) % width) for z in range(depth) for y in range(width)
        ]
        held = [(0, tuple(lax.ppermute(part, "mlp", route) for part in mine))]
        bit = sharers // 2
        while bit:
            swap = [(i, i ^ bit) for i in range(sharers)]
            held += [
                (flip ^ bit, tuple(lax.ppermute(part, "req", swap) for part in piece))
                for flip, piece in held
            ]
            bit //= 2
        flips = [flip for flip, _ in held]
        sides.append([piece for _, piece in held])
    return sides, flips


def cached_state(prefix_state, prefix_norm, prefix_owner, fd):
    heads, feats, hd = prefix_state.shape[1:]
    both = jnp.concatenate([prefix_state[0], prefix_norm[0][:, :, None]], axis=2).astype(BF16)
    ordered = jnp.concatenate([both[:, 1 + fd :], both[:, 1 : 1 + fd], both[:, :1]], axis=1)
    packed = jnp.pad(ordered, ((0, 0), (0, 15), (0, 128 - hd - 1)))
    slots = lax.axis_size("req")
    me = lax.axis_index("req")
    owner = prefix_owner[me]
    chosen = packed
    for turn in range(1, slots):
        other = lax.ppermute(packed, "req", [(i, i ^ turn) for i in range(slots)])
        chosen = jnp.where((me ^ turn) == owner, other, chosen)
    return chosen


def shards(
    residual_in,
    query_in,
    key_in,
    values_in,
    conv_weight,
    prefix_state,
    prefix_norm,
    prefix_owner,
    lengths,
    old_flags,
    out_weight,
    mlp_gain,
    gate_weight,
    up_weight,
    down_weight,
    next_gain,
    qkv_weight,
):
    mlp_count = lax.axis_size("mlp")
    column = lax.axis_index("mlp")
    width = mlp_count // DEPTH
    level = column // width
    heads = prefix_state.shape[1]
    hd = values_in.shape[1] // (heads * mlp_count)
    fd = query_in.shape[1] // (heads * mlp_count)

    state = cached_state(prefix_state, prefix_norm, prefix_owner, fd)
    pieces, flips = side_weights(gate_weight, up_weight, down_weight, width)

    taps = lax.dynamic_slice_in_dim(conv_weight, column * heads * hd, heads * hd, 1).T
    meta = jnp.concatenate([lengths, old_flags], axis=0)
    by_head = lax.all_to_all(pack(query_in, key_in, values_in, mlp_count), "mlp", 0, 0, tiled=True)
    attended = attention(meta, by_head, taps, state, heads, fd, hd)
    by_row = lax.all_to_all(attended, "mlp", 0, 0, tiled=True)
    by_row = by_row.reshape(mlp_count * heads * hd, by_row.shape[2])
    first_sum, normed = project(by_row, out_weight, residual_in, mlp_gain[None])

    def along(data, hops):
        return lax.ppermute(
            data, "mlp", [(a * width + y, b * width + y) for a, b in hops for y in range(width)]
        )

    own = (gate_weight, up_weight, down_weight)
    feed = lambda *xs: mlp(xs, own, pieces, flips)
    from_left = along(normed, [(0, 1), (1, 2), (2, 3)])
    from_right = along(normed, [(3, 2), (2, 1), (1, 0)])
    left_two = along(from_left, [(1, 2), (2, 3)])
    right_two = along(from_right, [(2, 1), (1, 0)])
    two = jnp.where(level >= 2, left_two, right_two)
    three = along(two, [(2, 3), (1, 0)])
    (part_own,) = feed(normed)
    part_left, part_right = feed(from_left, from_right)
    (part_two,) = feed(two)
    (part_three,) = feed(three)

    far = along(part_three, [(0, 1), (3, 2)])
    middle = part_two + far
    to_right = along(middle, [(0, 1), (1, 2)])
    to_left = along(middle, [(3, 2), (2, 1)])
    last_right = along(part_right + to_right, [(0, 1), (1, 2), (2, 3)])
    last_left = along(part_left + to_left, [(3, 2), (2, 1), (1, 0)])
    return next_projection(first_sum, part_own, last_right, last_left, next_gain[None], qkv_weight)


def solution(mesh):
    rows = P(("req", "mlp"), None)
    placed = (
        rows,
        rows,
        rows,
        rows,
        P(),
        P("req", "mlp", None, None),
        P("req", "mlp", None),
        P(),
        P("req", None),
        P("req", None),
        P(),
        P(),
        P(None, "mlp"),
        P(None, "mlp"),
        P("mlp", None),
        P(),
        P(),
    )
    return jax.shard_map(
        shards, mesh=mesh, in_specs=placed, out_specs=(rows, rows), check_vma=False
    )
```

```python
import functools
import math

import jax
import jax.numpy as jnp
from jax import lax
from jax.experimental import pallas as pl
from jax.experimental.pallas import tpu as pltpu
from jax.sharding import PartitionSpec as P

EPSILON = 1e-05
DEPTH = 4
TURNED = (((1,), (1,)), ((), ()))
MIB = 1 << 20
ACROSS = (((0,), (0,)), ((), ()))
PLAIN = (((1,), (0,)), ((), ()))
F32 = jnp.float32
BF16 = jnp.bfloat16
VMEM = pltpu.VMEM


def vmem():
    return pl.BlockSpec(memory_space=VMEM)


def dot(a, b, dims=PLAIN):
    return lax.dot_general(a, b, dims, preferred_element_type=F32)


def pack_kernel(q_ref, k_ref, v_ref, out_ref):
    count = out_ref.shape[0]
    at = 0
    for ref in (q_ref, k_ref, v_ref):
        turned = ref[...].T
        part = turned.shape[0] // count
        for m in range(count):
            out_ref[m, at : at + part, :] = turned[m * part : (m + 1) * part, :]
        at += part


def pack(q, k, v, count):
    rows = (q.shape[1] + k.shape[1] + v.shape[1]) // count
    return pl.pallas_call(
        pack_kernel,
        out_shape=jax.ShapeDtypeStruct((count, rows, q.shape[0]), BF16),
        in_specs=[vmem()] * 3,
        out_specs=vmem(),
        compiler_params=pltpu.CompilerParams(vmem_limit_bytes=24 * MIB),
        name="pack_heads",
    )(q, k, v)


def attention_kernel(heads, fd, hd, turns, *refs):
    lengths_ref, flags_ref, owner_ref, x_ref, conv_ref = refs[:5]
    states = refs[5 : 5 + len(turns)]
    out_ref, turned, vconv, feats, taps, cached = refs[5 + len(turns) :]
    blocks, rows, local = x_ref.shape
    tokens = blocks * local
    values_at = 2 * heads * fd
    tile = 256 if tokens % 256 == 0 else local
    slot = lax.axis_index("req")
    owner = owner_ref[slot]
    for turn, state in zip(turns, states):

        @pl.when((slot ^ turn) == owner)
        def _():
            cached[...] = state[...]

    for m in range(blocks):
        turned[:, m * local : (m + 1) * local] = x_ref[m]

    position = lax.broadcasted_iota(jnp.int32, (1, tokens), 1)
    start = jnp.zeros((1, tokens), jnp.int32)
    flag = jnp.zeros((1, tokens), F32) + flags_ref[0, 0].astype(F32)
    boundary = jnp.int32(0)
    for r in range(1, lengths_ref.shape[1]):
        boundary = boundary + lengths_ref[0, r - 1]
        reached = position >= boundary
        start = jnp.where(reached, boundary, start)
        flag = jnp.where(reached, flags_ref[0, r].astype(F32), flag)

    count = conv_ref.shape[0]
    spare = jnp.zeros((8 - count, conv_ref.shape[1]), F32)
    taps[...] = jnp.concatenate([conv_ref[...], spare], axis=0).T
    mine = pl.multiple_of(lax.axis_index("mlp") * heads * hd, 8)
    weights = taps[pl.ds(mine, heads * hd), :]
    values = turned[values_at:, :].astype(F32)
    total = weights[:, 0:1] * values
    for tap in range(1, count):
        earlier = pltpu.roll(values, tap, 1)
        total = total + weights[:, tap : tap + 1] * jnp.where(position - tap >= start, earlier, 0.0)
    vconv[...] = total.astype(BF16)

    for h in range(heads):
        query = turned[h * fd : (h + 1) * fd, :]
        wide = query.astype(F32)
        scaled = wide * (1.0 / math.sqrt(2.0 * fd))
        for a in range(fd):
            feats[a * fd : (a + 1) * fd, :] = (wide[a : a + 1, :] * scaled).astype(BF16)
        feats[fd * fd : fd * fd + fd, :] = (wide * fd ** (-0.25)).astype(BF16)
        ones = lax.broadcasted_iota(jnp.int32, (16, tokens), 0) == 0
        feats[fd * fd + fd :, :] = ones.astype(F32).astype(BF16)
        key = turned[(heads + h) * fd : (heads + h + 1) * fd, :]
        for first in range(0, tokens, tile):
            last = first + tile
            old = dot(cached[h], feats[:, first:last], ACROSS)
            score = dot(key[:, :last], query[:, first:last], ACROSS) * (fd**-0.5) + 1.0
            score = score * score * 0.5 + 0.5
            key_at = lax.broadcasted_iota(jnp.int32, (last, tile), 0)
            visible = (key_at >= start[:, first:last]) & (key_at <= position[:, first:last])
            score = jnp.where(visible, score, 0.0)
            den = jnp.sum(score, axis=0, keepdims=True) + flag[:, first:last] * old[hd : hd + 1, :]
            num = dot(vconv[h * hd : (h + 1) * hd, :last], score.astype(BF16))
            num = num + flag[:, first:last] * old[:hd, :]
            result = (num / den).astype(BF16)
            for at in range(first, last, local):
                out_ref[at // local, h * hd : (h + 1) * hd, :] = result[:, at - first : at - first + local]


def attention(lengths, flags, owner, x, conv, states, heads, fd, hd):
    blocks, rows, local = x.shape
    tokens = blocks * local
    turns = tuple(turn for turn, _ in states)
    arrays = [state for _, state in states]
    return pl.pallas_call(
        functools.partial(attention_kernel, heads, fd, hd, turns),
        out_shape=jax.ShapeDtypeStruct((blocks, heads * hd, local), BF16),
        in_specs=[pl.BlockSpec(memory_space=pltpu.SMEM)] * 3 + [vmem()] * (2 + len(arrays)),
        out_specs=vmem(),
        scratch_shapes=[
            VMEM((rows, tokens), BF16),
            VMEM((heads * hd, tokens), BF16),
            VMEM((arrays[0].shape[1], tokens), BF16),
            VMEM((conv.shape[1], 8), F32),
            VMEM(arrays[0].shape, BF16),
        ],
        compiler_params=pltpu.CompilerParams(vmem_limit_bytes=24 * MIB),
        name="attention",
    )(lengths, flags, owner, x, conv, *arrays)


def rms(rows, gain):
    return rows * lax.rsqrt(jnp.mean(rows * rows, axis=-1, keepdims=True) + EPSILON) * gain


def project_kernel(tile, att_ref, w_ref, res_ref, gain_ref, sum_ref, normed_ref, rows):
    step = pl.program_id(0)

    @pl.when(step == 0)
    def _():
        rows[...] = att_ref[...].T

    at = pl.ds(pl.multiple_of(step * tile, tile), tile)
    projected = dot(rows[...], w_ref[...])
    sum_ref[:, at] = (res_ref[:, at].astype(F32) + projected).astype(BF16)

    @pl.when(step == pl.num_programs(0) - 1)
    def _():
        normed_ref[...] = rms(sum_ref[...].astype(F32), gain_ref[...]).astype(BF16)


def project(att, w, residual, gain):
    depth, rows = att.shape
    width = w.shape[1]
    tile = 256
    whole = lambda shape: pl.BlockSpec(shape, lambda i: (0, 0))
    return pl.pallas_call(
        functools.partial(project_kernel, tile),
        grid=(width // tile,),
        out_shape=[jax.ShapeDtypeStruct((rows, width), BF16)] * 2,
        in_specs=[
            whole((depth, rows)),
            pl.BlockSpec((depth, tile), lambda i: (0, i)),
            whole((rows, width)),
            whole((1, width)),
        ],
        out_specs=[whole((rows, width))] * 2,
        scratch_shapes=[VMEM((rows, depth), BF16)],
        compiler_params=pltpu.CompilerParams(vmem_limit_bytes=24 * MIB),
        name="out_projection",
    )(att, w, residual, gain)


def mlp_kernel(inputs, *refs):
    xs, weights, outs = refs[:inputs], refs[inputs:-inputs], refs[-inputs:]
    x = xs[0][...] if inputs == 1 else jnp.concatenate([ref[...] for ref in xs], axis=0)
    total = None
    for at in range(0, len(weights), 3):
        gate_ref, up_ref, down_ref = weights[at : at + 3]
        gate = dot(x, gate_ref[...], TURNED)
        up = dot(x, up_ref[...], TURNED)
        hidden = (gate * jax.nn.sigmoid(gate) * up).astype(BF16)
        part = dot(hidden, down_ref[...])
        total = part if total is None else total + part
    local = xs[0].shape[0]
    for i, out in enumerate(outs):
        out[...] = total[i * local : (i + 1) * local].astype(BF16)


def mlp(xs, weights):
    rows, deep = xs[0].shape
    units = sum(w.shape[0] for w in weights) // 3
    return pl.pallas_call(
        functools.partial(mlp_kernel, len(xs)),
        out_shape=[jax.ShapeDtypeStruct((rows, deep), BF16)] * len(xs),
        in_specs=[vmem()] * (len(xs) + len(weights)),
        out_specs=[vmem()] * len(xs),
        compiler_params=pltpu.CompilerParams(vmem_limit_bytes=30 * MIB),
        cost_estimate=pl.CostEstimate(
            flops=6 * len(xs) * rows * deep * units,
            bytes_accessed=6 * deep * units,
            transcendentals=0,
        ),
        name="feed_forward",
    )(*xs, *weights)


def next_kernel(count, *refs):
    first_ref, parts = refs[0], refs[1 : 1 + count]
    gain_ref, w_ref, sum_ref, out_ref, normed = refs[1 + count :]
    step = pl.program_id(0)

    @pl.when(step == 0)
    def _():
        extra = sum(ref[...].astype(F32) for ref in parts)
        second = (first_ref[...].astype(F32) + extra).astype(BF16)
        sum_ref[...] = second
        normed[...] = rms(second.astype(F32), gain_ref[...]).astype(BF16)

    out_ref[...] = dot(normed[...], w_ref[...]).astype(BF16)


def next_projection(first, parts, gain, w):
    rows, deep = first.shape
    width = w.shape[1]
    tile = 256
    whole = lambda shape: pl.BlockSpec(shape, lambda i: (0, 0))
    return pl.pallas_call(
        functools.partial(next_kernel, len(parts)),
        grid=(width // tile,),
        out_shape=[
            jax.ShapeDtypeStruct((rows, deep), BF16),
            jax.ShapeDtypeStruct((rows, width), BF16),
        ],
        in_specs=[whole((rows, deep))] * (1 + len(parts))
        + [whole((1, deep)), pl.BlockSpec((deep, tile), lambda i: (0, i))],
        out_specs=[whole((rows, deep)), pl.BlockSpec((rows, tile), lambda i: (0, i))],
        scratch_shapes=[VMEM((rows, deep), BF16)],
        compiler_params=pltpu.CompilerParams(vmem_limit_bytes=24 * MIB),
        name="next_projection",
    )(first, *parts, gain, w)


def portion_kernel(gate, up, down, gate_out, up_out, down_out, sems):
    sharer = lax.axis_index("req")
    tall = gate_out.shape[0]
    wanted = sharer * tall
    first = jnp.minimum(wanted, gate.shape[0] - tall)
    rows = pl.ds(pl.multiple_of(first, 16), tall)
    copies = [
        pltpu.make_async_copy(ref.at[rows], out, sems.at[i])
        for i, (ref, out) in enumerate(((gate, gate_out), (up, up_out), (down, down_out)))
    ]
    for copy in copies:
        copy.start()
    for copy in copies:
        copy.wait()

    @pl.when(wanted > first)
    def _():
        spare = first + lax.broadcasted_iota(jnp.int32, (tall, 1), 0) < wanted
        for out in (gate_out, up_out, down_out):
            out[...] = jnp.where(spare, 0.0, out[...].astype(F32)).astype(BF16)


def portion(weights, sharers):
    units, deep = weights[0].shape
    tall = -(-units // (16 * sharers)) * 16
    return pl.pallas_call(
        portion_kernel,
        out_shape=[jax.ShapeDtypeStruct((tall, deep), BF16)] * 3,
        in_specs=[pl.BlockSpec(memory_space=pl.ANY)] * 3,
        out_specs=[vmem()] * 3,
        scratch_shapes=[pltpu.SemaphoreType.DMA((3,))],
        compiler_params=pltpu.CompilerParams(vmem_limit_bytes=16 * MIB),
        name="weight_share",
    )(*weights)


def partner_weights(mine, width):
    sharers = lax.axis_size("req")
    route = [(z * width + y, (z ^ 1) * width + y) for z in range(DEPTH) for y in range(width)]
    fetched = []
    for part in mine:
        if fetched:
            part, _ = lax.optimization_barrier((part, fetched[-1]))
        fetched.append(lax.ppermute(part, "mlp", route))
    whole = []
    for part in fetched:
        held = [part]
        bit = sharers // 2
        while bit:
            swap = [(i, i ^ bit) for i in range(sharers)]
            held += [lax.ppermute(piece, "req", swap) for piece in held]
            bit //= 2
        whole.append(jnp.concatenate(held, axis=0))
    return whole


def cached_state(prefix_state, prefix_norm, fd):
    heads, feats, hd = prefix_state.shape[1:]
    both = jnp.concatenate([prefix_state[0], prefix_norm[0][:, :, None]], axis=2).astype(BF16)
    ordered = jnp.concatenate([both[:, 1 + fd :], both[:, 1 : 1 + fd], both[:, :1]], axis=1)
    packed = jnp.pad(ordered, ((0, 0), (0, 15), (0, 128 - hd - 1)))
    return packed


def spread_state(packed):
    slots = lax.axis_size("req")
    states = [(0, packed)]
    for turn in range(1, slots):
        states.append((turn, lax.ppermute(packed, "req", [(i, i ^ turn) for i in range(slots)])))
    return states


def shards(
    residual_in,
    query_in,
    key_in,
    values_in,
    conv_weight,
    prefix_state,
    prefix_norm,
    prefix_owner,
    lengths,
    old_flags,
    out_weight,
    mlp_gain,
    gate_weight,
    up_weight,
    down_weight,
    next_gain,
    qkv_weight,
):
    mlp_count = lax.axis_size("mlp")
    width = mlp_count // DEPTH
    heads = prefix_state.shape[1]
    hd = values_in.shape[1] // (heads * mlp_count)
    fd = query_in.shape[1] // (heads * mlp_count)
    own = [gate_weight.T, up_weight.T, down_weight]

    packed = cached_state(prefix_state, prefix_norm, fd)
    share = portion(own, lax.axis_size("req"))
    query_in, packed, *share = lax.optimization_barrier((query_in, packed, *share))
    states = spread_state(packed)
    by_head = lax.all_to_all(pack(query_in, key_in, values_in, mlp_count), "mlp", 0, 0, tiled=True)
    weights = own + partner_weights(share, width)
    attended = attention(
        lengths, old_flags, prefix_owner, by_head, conv_weight, states, heads, fd, hd
    )
    by_row = lax.all_to_all(attended, "mlp", 0, 0, tiled=True)
    by_row = by_row.reshape(mlp_count * heads * hd, by_row.shape[2])
    first_sum, normed = project(by_row, out_weight, residual_in, mlp_gain[None])

    places = [(z, y) for z in range(DEPTH) for y in range(width)]

    def across(data):
        return lax.ppermute(data, "mlp", [(z * width + y, (z ^ 2) * width + y) for z, y in places])

    def beside(data, turn):
        return lax.ppermute(
            data, "mlp", [(z * width + y, z * width + (y + turn) % width) for z, y in places]
        )

    turns = range(1, width)
    far = across(normed)
    near = [beside(normed, turn) for turn in turns]
    part_own, *part_near = mlp([normed, *near], weights)
    far_near = [beside(far, turn) for turn in turns]
    (part_far,) = mlp([far], weights)
    part_far_near = mlp(far_near, weights)
    for turn, part in zip(turns, part_far_near):
        part_far = part_far.astype(F32) + beside(part, -turn).astype(F32)
    back = across(part_far.astype(BF16))
    near_back = [beside(part, -turn) for turn, part in zip(turns, part_near)]
    parts = [part_own, back, *near_back]
    return next_projection(first_sum, parts, next_gain[None], qkv_weight)


def solution(mesh):
    rows = P(("req", "mlp"), None)
    placed = (
        rows,
        rows,
        rows,
        rows,
        P(),
        P("req", "mlp", None, None),
        P("req", "mlp", None),
        P(),
        P("req", None),
        P("req", None),
        P(),
        P(),
        P(None, "mlp"),
        P(None, "mlp"),
        P("mlp", None),
        P(),
        P(),
    )
    return jax.shard_map(
        shards, mesh=mesh, in_specs=placed, out_specs=(rows, rows), check_vma=False
    )
```

```python
import functools
import math

import jax
import jax.numpy as jnp
from jax import lax
from jax.experimental import pallas as pl
from jax.experimental.pallas import tpu as pltpu
from jax.sharding import PartitionSpec as P

EPSILON = 1e-05
DEPTH = 4
TURNED = (((1,), (1,)), ((), ()))
MIB = 1 << 20
ACROSS = (((0,), (0,)), ((), ()))
PLAIN = (((1,), (0,)), ((), ()))
F32 = jnp.float32
BF16 = jnp.bfloat16
VMEM = pltpu.VMEM
GRANT = 60 * MIB
FRONT = 60
PARTS = 2
LIGHT = pl.CostEstimate(flops=1, bytes_accessed=1, transcendentals=0)


def vmem():
    return pl.BlockSpec(memory_space=VMEM)


def dot(a, b, dims=PLAIN):
    return lax.dot_general(a, b, dims, preferred_element_type=F32)


def hbm():
    return pl.BlockSpec(memory_space=pltpu.HBM)


def stay(x):
    return pltpu.with_memory_space_constraint(x, pltpu.HBM)


def pack_kernel(q_hbm, k_hbm, v_hbm, out_hbm, q, k, v, out, sems):
    count = out.shape[0]
    loads = [
        pltpu.make_async_copy(src, dst, sems.at[i])
        for i, (src, dst) in enumerate(((q_hbm, q), (k_hbm, k), (v_hbm, v)))
    ]
    for load in loads:
        load.start()
    at = 0
    for load, ref in zip(loads, (q, k, v)):
        load.wait()
        part = ref.shape[1] // count
        turned = ref[...].T
        for m in range(count):
            out[m, at : at + part, :] = turned[m * part : (m + 1) * part, :]
        at += part
    store = pltpu.make_async_copy(out, out_hbm, sems.at[3])
    store.start()
    store.wait()


def pack(q, k, v, count):
    rows = (q.shape[1] + k.shape[1] + v.shape[1]) // count
    shape = (count, rows, q.shape[0])
    return pl.pallas_call(
        pack_kernel,
        out_shape=jax.ShapeDtypeStruct(shape, BF16),
        in_specs=[hbm()] * 3,
        out_specs=hbm(),
        scratch_shapes=[
            VMEM(q.shape, BF16),
            VMEM(k.shape, BF16),
            VMEM(v.shape, BF16),
            VMEM(shape, BF16),
            pltpu.SemaphoreType.DMA((4,)),
        ],
        compiler_params=pltpu.CompilerParams(vmem_limit_bytes=24 * MIB),
        cost_estimate=LIGHT,
        name="pack_heads",
    )(stay(q), stay(k), stay(v))


def attention_kernel(heads, fd, hd, turns, *refs):
    lengths_ref, flags_ref, owner_ref, conv_ref = refs[:4]
    states, refs = refs[4 : 4 + len(turns)], refs[4 + len(turns) :]
    x_hbm, out_hbm, turned, vconv, feats, taps, cached, out_ref, in_sems, state_sem, out_sems = refs
    blocks, rows, local = x_hbm.shape
    tokens = blocks * local
    values_at = 2 * heads * fd
    tile = 256 if tokens % 256 == 0 else local
    me = lax.axis_index("mlp")
    loads = [
        pltpu.make_async_copy(x_hbm.at[m], turned.at[:, pl.ds(m * local, local)], in_sems.at[m])
        for m in range(blocks)
    ]
    for load in loads:
        load.start()
    slot = lax.axis_index("req")
    owner = owner_ref[slot]
    for turn, state in zip(turns, states):

        @pl.when((slot ^ turn) == owner)
        def _():
            pltpu.make_async_copy(state, cached, state_sem).start()

    position = lax.broadcasted_iota(jnp.int32, (1, tokens), 1)
    start = jnp.zeros((1, tokens), jnp.int32)
    flag = jnp.zeros((1, tokens), F32) + flags_ref[0, 0].astype(F32)
    boundary = jnp.int32(0)
    for r in range(1, lengths_ref.shape[1]):
        boundary = boundary + lengths_ref[0, r - 1]
        reached = position >= boundary
        start = jnp.where(reached, boundary, start)
        flag = jnp.where(reached, flags_ref[0, r].astype(F32), flag)

    count = conv_ref.shape[0]
    spare = jnp.zeros((8 - count, conv_ref.shape[1]), F32)
    taps[...] = jnp.concatenate([conv_ref[...], spare], axis=0).T
    mine = pl.multiple_of(me * heads * hd, 8)
    weights = taps[pl.ds(mine, heads * hd), :]
    for load in loads:
        load.wait()
    values = turned[values_at:, :].astype(F32)
    total = weights[:, 0:1] * values
    for tap in range(1, count):
        earlier = pltpu.roll(values, tap, 1)
        total = total + weights[:, tap : tap + 1] * jnp.where(position - tap >= start, earlier, 0.0)
    vconv[...] = total.astype(BF16)

    for h in range(heads):
        wide = turned[h * fd : (h + 1) * fd, :].astype(F32)
        scaled = wide * (1.0 / math.sqrt(2.0 * fd))
        for a in range(fd):
            feats[h, a * fd : (a + 1) * fd, :] = (wide[a : a + 1, :] * scaled).astype(BF16)
        feats[h, fd * fd : fd * fd + fd, :] = (wide * fd ** (-0.25)).astype(BF16)
        ones = lax.broadcasted_iota(jnp.int32, (16, tokens), 0) == 0
        feats[h, fd * fd + fd :, :] = ones.astype(F32).astype(BF16)
    pltpu.make_async_copy(states[0], cached, state_sem).wait()
    stores = []
    for first in range(0, tokens, tile):
        last = first + tile
        flags = flag[:, first:last]
        key_at = lax.broadcasted_iota(jnp.int32, (last, tile), 0)
        visible = (key_at >= start[:, first:last]) & (key_at <= position[:, first:last])
        for h in range(heads):
            key = turned[(heads + h) * fd : (heads + h + 1) * fd, :last]
            old = dot(cached[h], feats[h, :, first:last], ACROSS)
            score = dot(key, turned[h * fd : (h + 1) * fd, first:last], ACROSS) * (fd**-0.5) + 1.0
            score = jnp.where(visible, score * score * 0.5 + 0.5, 0.0)
            den = jnp.sum(score, axis=0, keepdims=True) + flags * old[hd : hd + 1, :]
            num = dot(vconv[h * hd : (h + 1) * hd, :last], score.astype(BF16))
            result = ((num + flags * old[:hd, :]) / den).astype(BF16)
            for at in range(first, last, local):
                out_ref[at // local, h * hd : (h + 1) * hd, :] = result[:, at - first : at - first + local]
        for m in range(first // local, last // local):
            stores.append(pltpu.make_async_copy(out_ref.at[m], out_hbm.at[m], out_sems.at[m]))
            stores[-1].start()
    for store in stores:
        store.wait()


def attention(lengths, flags, owner, x, conv, states, heads, fd, hd):
    blocks, rows, local = x.shape
    tokens = blocks * local
    turns = tuple(turn for turn, _ in states)
    arrays = [state for _, state in states]
    return pl.pallas_call(
        functools.partial(attention_kernel, heads, fd, hd, turns),
        out_shape=jax.ShapeDtypeStruct((blocks, heads * hd, local), BF16),
        in_specs=[pl.BlockSpec(memory_space=pltpu.SMEM)] * 3
        + [vmem()]
        + [hbm()] * (len(arrays) + 1),
        out_specs=hbm(),
        scratch_shapes=[
            VMEM((rows, tokens), BF16),
            VMEM((heads * hd, tokens), BF16),
            VMEM((heads, arrays[0].shape[1], tokens), BF16),
            VMEM((conv.shape[1], 8), F32),
            VMEM(arrays[0].shape, BF16),
            VMEM((blocks, heads * hd, local), BF16),
            pltpu.SemaphoreType.DMA((blocks,)),
            pltpu.SemaphoreType.DMA,
            pltpu.SemaphoreType.DMA((blocks,)),
        ],
        compiler_params=pltpu.CompilerParams(vmem_limit_bytes=GRANT),
        cost_estimate=LIGHT,
        name="attention",
    )(lengths, flags, owner, conv, *arrays, x)


def rms(rows, gain):
    return rows * lax.rsqrt(jnp.mean(rows * rows, axis=-1, keepdims=True) + EPSILON) * gain


def project_kernel(att_hbm, w_hbm, res_hbm, gain_ref, sum_ref, normed_ref, *refs):
    halves, (att, res, w, sems) = refs[:-4], refs[-4:]
    loads = [
        pltpu.make_async_copy(src, dst, sems.at[i])
        for i, (src, dst) in enumerate(((att_hbm, att), (w_hbm, w), (res_hbm, res)))
    ]
    for load in loads:
        load.start()
    for load in loads:
        load.wait()
    summed = (res[...].astype(F32) + dot(att[...].T, w[...])).astype(BF16)
    sum_ref[...] = summed
    normed = rms(summed.astype(F32), gain_ref[0:1, :]).astype(BF16)
    normed_ref[...] = normed
    step = halves[0].shape[0]
    for i, half in enumerate(halves):
        half[...] = normed[i * step : (i + 1) * step]


def project(att, w, residual, gains):
    rows = att.shape[1]
    width = w.shape[1]
    full = jax.ShapeDtypeStruct((rows, width), BF16)
    part = jax.ShapeDtypeStruct((rows // PARTS, width), BF16)
    first_sum, normed, *halves = pl.pallas_call(
        project_kernel,
        out_shape=[full] * 2 + [part] * PARTS,
        in_specs=[hbm()] * 3 + [vmem()],
        out_specs=[vmem()] * (2 + PARTS),
        scratch_shapes=[
            VMEM(att.shape, BF16),
            VMEM(residual.shape, BF16),
            VMEM(w.shape, BF16),
            pltpu.SemaphoreType.DMA((3,)),
        ],
        compiler_params=pltpu.CompilerParams(vmem_limit_bytes=40 * MIB),
        cost_estimate=LIGHT,
        name="out_projection",
    )(att, stay(w), stay(residual), gains)
    return first_sum, normed, halves


def mlp_kernel(inputs, flips, sharers, *refs):
    xs, own, refs = refs[:inputs], refs[inputs : inputs + 3], refs[inputs + 3 :]
    pieces, outs = refs[:-inputs], refs[-inputs:]
    x = xs[0][...] if inputs == 1 else jnp.concatenate([ref[...] for ref in xs], axis=0)
    units = own[0].shape[0]
    tall, sizes = share_of(units, sharers)
    column = lax.broadcasted_iota(jnp.int32, (1, sum(ref.shape[1] for ref in pieces)), 1)
    fresh, at = column * 0, 0
    for part, flip in flips:
        sharer = lax.axis_index("req") ^ flip
        repeated = sharer * tall - first_unit(sharer, tall, units) - sum(sizes[:part])
        fresh = jnp.where(column >= at, at + repeated, fresh)
        at += sizes[part]
    total = None
    for gates, ups, downs in ([[ref] for ref in own], [[ref.at[i] for ref in pieces] for i in range(3)]):
        gate, up = (
            dot(x, jnp.concatenate([ref[...] for ref in group], axis=0), TURNED)
            for group in (gates, ups)
        )
        hidden = gate * jax.nn.sigmoid(gate) * up
        if gates[0] is not own[0]:
            hidden = jnp.where(column >= fresh, hidden, 0.0)
        part = dot(hidden.astype(BF16), jnp.concatenate([ref[...] for ref in downs], axis=0))
        total = part if total is None else total + part
    local = xs[0].shape[0]
    for i, out in enumerate(outs):
        out[...] = total[i * local : (i + 1) * local].astype(BF16)


def mlp(xs, own, pieces):
    rows, deep = xs[0].shape
    flips = [flip for flip, _ in pieces]
    return pl.pallas_call(
        functools.partial(mlp_kernel, len(xs), flips, lax.axis_size("req")),
        out_shape=[jax.ShapeDtypeStruct((rows, deep), BF16)] * len(xs),
        in_specs=[vmem()] * (len(xs) + 3 + len(pieces)),
        out_specs=[vmem()] * len(xs),
        compiler_params=pltpu.CompilerParams(vmem_limit_bytes=30 * MIB),
        cost_estimate=LIGHT,
        name="feed_forward",
    )(*xs, *own, *(piece for _, piece in pieces))


def add_kernel(*refs):
    refs[-1][...] = sum(ref[...].astype(F32) for ref in refs[:-1]).astype(BF16)


def add(parts):
    return pl.pallas_call(
        add_kernel,
        out_shape=jax.ShapeDtypeStruct(parts[0].shape, BF16),
        in_specs=[vmem()] * len(parts),
        out_specs=vmem(),
        compiler_params=pltpu.CompilerParams(vmem_limit_bytes=16 * MIB),
        cost_estimate=LIGHT,
        name="add_parts",
    )(*parts)


def next_kernel(whole, *refs):
    first_ref, wholes, halves = refs[0], refs[1 : 1 + whole], refs[1 + whole : -6]
    gain_ref, w_hbm, sum_ref, out_ref, w, w_sem = refs[-6:]
    load = pltpu.make_async_copy(w_hbm, w, w_sem)
    load.start()
    extra = sum(ref[...].astype(F32) for ref in wholes)
    extra = extra + jnp.concatenate([ref[...].astype(F32) for ref in halves], axis=0)
    second = (first_ref[...].astype(F32) + extra).astype(BF16)
    sum_ref[...] = second
    normed = rms(second.astype(F32), gain_ref[1:2, :]).astype(BF16)
    load.wait()
    out_ref[...] = dot(normed, w[...]).astype(BF16)


def next_projection(first, wholes, halves, gains, w):
    rows, deep = first.shape
    width = w.shape[1]
    return pl.pallas_call(
        functools.partial(next_kernel, len(wholes)),
        out_shape=[
            jax.ShapeDtypeStruct((rows, deep), BF16),
            jax.ShapeDtypeStruct((rows, width), BF16),
        ],
        in_specs=[vmem()] * (2 + len(wholes) + len(halves)) + [hbm()],
        out_specs=[vmem()] * 2,
        scratch_shapes=[VMEM(w.shape, BF16), pltpu.SemaphoreType.DMA],
        compiler_params=pltpu.CompilerParams(vmem_limit_bytes=40 * MIB),
        cost_estimate=LIGHT,
        name="next_projection",
    )(first, *wholes, *halves, gains, w)


def share_of(units, sharers):
    tall = -(-units // (16 * sharers)) * 16
    if tall < 64:
        return tall, [tall]
    front = -(-tall * FRONT // 1600) * 16
    return tall, [front, tall - front]


def first_unit(sharer, tall, units):
    return jnp.minimum(sharer * tall, units - tall)


def portion_kernel(gate, up, down, *refs):
    outs, sems = refs[:-1], refs[-1]
    tall = sum(out.shape[1] for out in outs)
    at = first_unit(lax.axis_index("req"), tall, gate.shape[0])
    copies = []
    for out in outs:
        rows = pl.ds(pl.multiple_of(at, 16), out.shape[1])
        for i, ref in enumerate((gate, up, down)):
            copies.append(pltpu.make_async_copy(ref.at[rows], out.at[i], sems.at[len(copies)]))
        at = at + out.shape[1]
    for copy in copies:
        copy.start()
    for copy in copies:
        copy.wait()


def portion(weights, sharers):
    units, deep = weights[0].shape
    sizes = share_of(units, sharers)[1]
    return pl.pallas_call(
        portion_kernel,
        out_shape=[jax.ShapeDtypeStruct((3, size, deep), BF16) for size in sizes],
        in_specs=[hbm()] * 3,
        out_specs=[hbm()] * len(sizes),
        scratch_shapes=[pltpu.SemaphoreType.DMA((3 * len(sizes),))],
        compiler_params=pltpu.CompilerParams(vmem_limit_bytes=16 * MIB),
        cost_estimate=LIGHT,
        name="weight_share",
    )(*(stay(w) for w in weights))


def from_line(part, width):
    return [
        lax.ppermute(
            part,
            "mlp",
            [(z * width + y, z * width + (y + turn) % width) for z in range(DEPTH) for y in range(width)],
        )
        for turn in range(1, width)
    ]


def swapped(part, bit):
    return lax.ppermute(part, "req", [(i, i ^ bit) for i in range(lax.axis_size("req"))])


def by_xor(blocks, axis):
    count = lax.axis_size(axis)
    return [blocks[0]] + [
        lax.ppermute(blocks[turn], axis, [(i, i ^ turn) for i in range(count)])
        for turn in range(1, count)
    ]


def after(values, *earlier):
    values, _ = lax.optimization_barrier((values, earlier))
    return values


def cached_state(prefix_state, prefix_norm, fd):
    heads, feats, hd = prefix_state.shape[1:]
    both = jnp.concatenate([prefix_state[0], prefix_norm[0][:, :, None]], axis=2).astype(BF16)
    ordered = jnp.concatenate([both[:, 1 + fd :], both[:, 1 : 1 + fd], both[:, :1]], axis=1)
    packed = jnp.pad(ordered, ((0, 0), (0, 15), (0, 128 - hd - 1)))
    return packed


def shards(
    residual_in,
    query_in,
    key_in,
    values_in,
    conv_weight,
    prefix_state,
    prefix_norm,
    prefix_owner,
    lengths,
    old_flags,
    out_weight,
    mlp_gain,
    gate_weight,
    up_weight,
    down_weight,
    next_gain,
    qkv_weight,
):
    mlp_count = lax.axis_size("mlp")
    width = mlp_count // DEPTH
    heads = prefix_state.shape[1]
    hd = values_in.shape[1] // (heads * mlp_count)
    fd = query_in.shape[1] // (heads * mlp_count)
    own = [gate_weight.T, up_weight.T, down_weight]

    sharers = lax.axis_size("req")
    packed = cached_state(prefix_state, prefix_norm, fd)
    gains = jnp.stack([mlp_gain, next_gain])
    states = list(enumerate(by_xor([packed] * sharers, "req")))
    tokens = pack(*after((query_in, key_in, values_in), packed, gains), mlp_count)
    by_head = lax.all_to_all(tokens, "mlp", 0, 0, tiled=True)
    share = portion(after(own, tokens), sharers)
    count = len(share)
    lines = [from_line(share[0], width)]
    by_head = after(by_head, share)
    attended = attention(
        lengths, old_flags, prefix_owner, by_head, conv_weight, states, heads, fd, hd
    )
    by_row = lax.all_to_all(attended, "mlp", 0, 0, tiled=True)
    by_row = by_row.reshape(mlp_count * heads * hd, by_row.shape[2])

    bits = [1 << i for i in reversed(range(sharers.bit_length() - 1))]

    def pass_on(held, bit):
        return held + [((part, flip ^ bit), swapped(piece, bit)) for (part, flip), piece in held]

    held = [((0, 0), piece) for piece in after(lines[0], attended)]
    for bit in bits[:-1]:
        held = pass_on(held, bit)
    for part in range(1, count):
        lines.append(from_line(after(share[part], lines[-1], attended), width))
    first_sum, normed, parts = project(after(by_row, lines[0]), out_weight, residual_in, gains)

    def across(data):
        return lax.ppermute(data, "mlp", [(i, (i + mlp_count // 2) % mlp_count) for i in range(mlp_count)])

    def beside(data):
        return lax.ppermute(data, "mlp", [(i, i ^ width) for i in range(mlp_count)])

    near = beside(normed)
    far = [across(parts[0])]
    pieces, near = after(([piece for _, piece in held], near), far[0])
    held = list(zip([key for key, _ in held], pieces))
    far_near = []
    for part, piece in enumerate(lines[1:], 1):
        rest = [((part, 0), one) for one in piece]
        for bit in bits[:-1]:
            rest = pass_on(rest, bit)
        held = held + rest
    for part in parts[1:]:
        sent = after(far[-1], near, *far_near)
        far.append(across(after(part, near, far)))
        far_near.append(beside(sent))
    far_near.append(beside(after(far[-1], far_near)))
    pieces = [(key, after(piece, far_near[0], far[-1])) for key, piece in held]
    pieces = pass_on(pieces, bits[-1])
    back, sums = [], []
    fed = []
    for pair in zip(far, far_near):
        fed.append(mlp(after(list(pair), fed), own, pieces))
    for kept, sent in fed:
        total = add([kept, beside(sent)])
        back.append(across(after(total, back)))
        sums.append(total)
    part_own, part_near = mlp(after([normed, near], sums[0]), own, pieces)
    near_back = beside(part_near)
    return next_projection(first_sum, [part_own, near_back], back, gains, qkv_weight)


def solution(mesh):
    rows = P(("req", "mlp"), None)
    placed = (
        rows,
        rows,
        rows,
        rows,
        P(),
        P("req", "mlp", None, None),
        P("req", "mlp", None),
        P(),
        P("req", None),
        P("req", None),
        P(),
        P(),
        P(None, "mlp"),
        P(None, "mlp"),
        P("mlp", None),
        P(),
        P(),
    )
    return jax.shard_map(
        shards, mesh=mesh, in_specs=placed, out_specs=(rows, rows), check_vma=False
    )
```

```python
import functools
import math

import jax
import jax.numpy as jnp
from jax import lax
from jax.experimental import pallas as pl
from jax.experimental.pallas import tpu as pltpu
from jax.sharding import PartitionSpec as P

EPSILON = 1e-05
DEPTH = 4
TURNED = (((1,), (1,)), ((), ()))
MIB = 1 << 20
ACROSS = (((0,), (0,)), ((), ()))
PLAIN = (((1,), (0,)), ((), ()))
F32 = jnp.float32
BF16 = jnp.bfloat16
VMEM = pltpu.VMEM
GRANT = 60 * MIB
FRONT = 60
PARTS = 2
LIGHT = pl.CostEstimate(flops=1, bytes_accessed=1, transcendentals=0)


def vmem():
    return pl.BlockSpec(memory_space=VMEM)


def dot(a, b, dims=PLAIN):
    return lax.dot_general(a, b, dims, preferred_element_type=F32)


def hbm():
    return pl.BlockSpec(memory_space=pltpu.HBM)


def stay(x):
    return pltpu.with_memory_space_constraint(x, pltpu.HBM)


def pack_kernel(q_hbm, k_hbm, v_hbm, out_hbm, q, k, v, out, sems):
    count = out.shape[0]
    loads = [
        pltpu.make_async_copy(src, dst, sems.at[i])
        for i, (src, dst) in enumerate(((q_hbm, q), (k_hbm, k), (v_hbm, v)))
    ]
    for load in loads:
        load.start()
    at = 0
    for load, ref in zip(loads, (q, k, v)):
        load.wait()
        part = ref.shape[1] // count
        turned = ref[...].T
        for m in range(count):
            out[m, at : at + part, :] = turned[m * part : (m + 1) * part, :]
        at += part
    store = pltpu.make_async_copy(out, out_hbm, sems.at[3])
    store.start()
    store.wait()


def pack(q, k, v, count):
    rows = (q.shape[1] + k.shape[1] + v.shape[1]) // count
    shape = (count, rows, q.shape[0])
    return pl.pallas_call(
        pack_kernel,
        out_shape=jax.ShapeDtypeStruct(shape, BF16),
        in_specs=[hbm()] * 3,
        out_specs=hbm(),
        scratch_shapes=[
            VMEM(q.shape, BF16),
            VMEM(k.shape, BF16),
            VMEM(v.shape, BF16),
            VMEM(shape, BF16),
            pltpu.SemaphoreType.DMA((4,)),
        ],
        compiler_params=pltpu.CompilerParams(vmem_limit_bytes=24 * MIB),
        cost_estimate=LIGHT,
        name="pack_heads",
    )(stay(q), stay(k), stay(v))


def attention_kernel(heads, fd, hd, turns, *refs):
    lengths_ref, flags_ref, owner_ref, conv_ref = refs[:4]
    states, refs = refs[4 : 4 + len(turns)], refs[4 + len(turns) :]
    x_hbm, out_hbm, turned, vconv, feats, taps, cached, out_ref, in_sems, state_sem, out_sems = refs
    blocks, rows, local = x_hbm.shape
    tokens = blocks * local
    values_at = 2 * heads * fd
    tile = 256 if tokens % 256 == 0 else local
    me = lax.axis_index("mlp")
    loads = [
        pltpu.make_async_copy(x_hbm.at[m], turned.at[:, pl.ds(m * local, local)], in_sems.at[m])
        for m in range(blocks)
    ]
    for load in loads:
        load.start()
    slot = lax.axis_index("req")
    owner = owner_ref[slot]
    for turn, state in zip(turns, states):

        @pl.when((slot ^ turn) == owner)
        def _():
            pltpu.make_async_copy(state, cached, state_sem).start()

    position = lax.broadcasted_iota(jnp.int32, (1, tokens), 1)
    start = jnp.zeros((1, tokens), jnp.int32)
    flag = jnp.zeros((1, tokens), F32) + flags_ref[0, 0].astype(F32)
    boundary = jnp.int32(0)
    for r in range(1, lengths_ref.shape[1]):
        boundary = boundary + lengths_ref[0, r - 1]
        reached = position >= boundary
        start = jnp.where(reached, boundary, start)
        flag = jnp.where(reached, flags_ref[0, r].astype(F32), flag)

    count = conv_ref.shape[0]
    spare = jnp.zeros((8 - count, conv_ref.shape[1]), F32)
    taps[...] = jnp.concatenate([conv_ref[...], spare], axis=0).T
    mine = pl.multiple_of(me * heads * hd, 8)
    weights = taps[pl.ds(mine, heads * hd), :]
    for load in loads:
        load.wait()
    values = turned[values_at:, :].astype(F32)
    total = weights[:, 0:1] * values
    for tap in range(1, count):
        earlier = pltpu.roll(values, tap, 1)
        total = total + weights[:, tap : tap + 1] * jnp.where(position - tap >= start, earlier, 0.0)
    vconv[...] = total.astype(BF16)

    for h in range(heads):
        wide = turned[h * fd : (h + 1) * fd, :].astype(F32)
        scaled = wide * (1.0 / math.sqrt(2.0 * fd))
        for a in range(fd):
            feats[h, a * fd : (a + 1) * fd, :] = (wide[a : a + 1, :] * scaled).astype(BF16)
        feats[h, fd * fd : fd * fd + fd, :] = (wide * fd ** (-0.25)).astype(BF16)
        ones = lax.broadcasted_iota(jnp.int32, (16, tokens), 0) == 0
        feats[h, fd * fd + fd :, :] = ones.astype(F32).astype(BF16)
    pltpu.make_async_copy(states[0], cached, state_sem).wait()
    stores = []
    for first in range(0, tokens, tile):
        last = first + tile
        flags = flag[:, first:last]
        key_at = lax.broadcasted_iota(jnp.int32, (last, tile), 0)
        visible = (key_at >= start[:, first:last]) & (key_at <= position[:, first:last])
        for h in range(heads):
            key = turned[(heads + h) * fd : (heads + h + 1) * fd, :last]
            old = dot(cached[h], feats[h, :, first:last], ACROSS)
            score = dot(key, turned[h * fd : (h + 1) * fd, first:last], ACROSS) * (fd**-0.5) + 1.0
            score = jnp.where(visible, score * score * 0.5 + 0.5, 0.0)
            den = jnp.sum(score, axis=0, keepdims=True) + flags * old[hd : hd + 1, :]
            num = dot(vconv[h * hd : (h + 1) * hd, :last], score.astype(BF16))
            result = ((num + flags * old[:hd, :]) / den).astype(BF16)
            for at in range(first, last, local):
                out_ref[at // local, h * hd : (h + 1) * hd, :] = result[:, at - first : at - first + local]
        for m in range(first // local, last // local):
            stores.append(pltpu.make_async_copy(out_ref.at[m], out_hbm.at[m], out_sems.at[m]))
            stores[-1].start()
    for store in stores:
        store.wait()


def attention(lengths, flags, owner, x, conv, states, heads, fd, hd):
    blocks, rows, local = x.shape
    tokens = blocks * local
    turns = tuple(turn for turn, _ in states)
    arrays = [state for _, state in states]
    return pl.pallas_call(
        functools.partial(attention_kernel, heads, fd, hd, turns),
        out_shape=jax.ShapeDtypeStruct((blocks, heads * hd, local), BF16),
        in_specs=[pl.BlockSpec(memory_space=pltpu.SMEM)] * 3
        + [vmem()]
        + [hbm()] * (len(arrays) + 1),
        out_specs=hbm(),
        scratch_shapes=[
            VMEM((rows, tokens), BF16),
            VMEM((heads * hd, tokens), BF16),
            VMEM((heads, arrays[0].shape[1], tokens), BF16),
            VMEM((conv.shape[1], 8), F32),
            VMEM(arrays[0].shape, BF16),
            VMEM((blocks, heads * hd, local), BF16),
            pltpu.SemaphoreType.DMA((blocks,)),
            pltpu.SemaphoreType.DMA,
            pltpu.SemaphoreType.DMA((blocks,)),
        ],
        compiler_params=pltpu.CompilerParams(vmem_limit_bytes=GRANT),
        cost_estimate=LIGHT,
        name="attention",
    )(lengths, flags, owner, conv, *arrays, x)


def rms(rows, gain):
    return rows * lax.rsqrt(jnp.mean(rows * rows, axis=-1, keepdims=True) + EPSILON) * gain


def project_kernel(att_hbm, w_hbm, res_hbm, gain_ref, sum_ref, normed_ref, *refs):
    halves, (att, res, w, sems) = refs[:-4], refs[-4:]
    half = w.shape[0] // 2
    loads = [
        pltpu.make_async_copy(src, dst, sems.at[i])
        for i, (src, dst) in enumerate(
            (
                (att_hbm, att),
                (w_hbm.at[pl.ds(0, half)], w.at[pl.ds(0, half)]),
                (w_hbm.at[pl.ds(half, half)], w.at[pl.ds(half, half)]),
                (res_hbm, res),
            )
        )
    ]
    for load in loads:
        load.start()
    loads[0].wait()
    rows = att[...].T
    loads[1].wait()
    projected = dot(rows[:, :half], w[:half, :])
    loads[2].wait()
    projected = projected + dot(rows[:, half:], w[half:, :])
    loads[3].wait()
    summed = (res[...].astype(F32) + projected).astype(BF16)
    sum_ref[...] = summed
    normed = rms(summed.astype(F32), gain_ref[...]).astype(BF16)
    normed_ref[...] = normed
    step = halves[0].shape[0]
    for i, half in enumerate(halves):
        half[...] = normed[i * step : (i + 1) * step]


def project(att, w, residual, gains):
    rows = att.shape[1]
    width = w.shape[1]
    full = jax.ShapeDtypeStruct((rows, width), BF16)
    part = jax.ShapeDtypeStruct((rows // PARTS, width), BF16)
    first_sum, normed, *halves = pl.pallas_call(
        project_kernel,
        out_shape=[full] * 2 + [part] * PARTS,
        in_specs=[hbm()] * 3 + [vmem()],
        out_specs=[vmem()] * (2 + PARTS),
        scratch_shapes=[
            VMEM(att.shape, BF16),
            VMEM(residual.shape, BF16),
            VMEM(w.shape, BF16),
            pltpu.SemaphoreType.DMA((4,)),
        ],
        compiler_params=pltpu.CompilerParams(vmem_limit_bytes=40 * MIB),
        cost_estimate=LIGHT,
        name="out_projection",
    )(att, stay(w), stay(residual), gains)
    return first_sum, normed, halves


def mlp_kernel(inputs, flips, sharers, *refs):
    xs, own, refs = refs[:inputs], refs[inputs : inputs + 3], refs[inputs + 3 :]
    pieces, outs = refs[:-inputs], refs[-inputs:]
    x = xs[0][...] if inputs == 1 else jnp.concatenate([ref[...] for ref in xs], axis=0)
    units = own[0].shape[0]
    tall, sizes = share_of(units, sharers)
    column = lax.broadcasted_iota(jnp.int32, (1, sum(ref.shape[1] for ref in pieces)), 1)
    fresh, at = column * 0, 0
    for part, flip in flips:
        sharer = lax.axis_index("req") ^ flip
        repeated = sharer * tall - first_unit(sharer, tall, units) - sum(sizes[:part])
        fresh = jnp.where(column >= at, at + repeated, fresh)
        at += sizes[part]
    total = None
    for gates, ups, downs in ([[ref] for ref in own], [[ref.at[i] for ref in pieces] for i in range(3)]):
        gate, up = (
            dot(x, jnp.concatenate([ref[...] for ref in group], axis=0), TURNED)
            for group in (gates, ups)
        )
        hidden = gate * jax.nn.sigmoid(gate) * up
        if gates[0] is not own[0]:
            hidden = jnp.where(column >= fresh, hidden, 0.0)
        part = dot(hidden.astype(BF16), jnp.concatenate([ref[...] for ref in downs], axis=0))
        total = part if total is None else total + part
    local = xs[0].shape[0]
    for i, out in enumerate(outs):
        out[...] = total[i * local : (i + 1) * local].astype(BF16)


def mlp(xs, own, pieces):
    rows, deep = xs[0].shape
    flips = [flip for flip, _ in pieces]
    return pl.pallas_call(
        functools.partial(mlp_kernel, len(xs), flips, lax.axis_size("req")),
        out_shape=[jax.ShapeDtypeStruct((rows, deep), BF16)] * len(xs),
        in_specs=[vmem()] * (len(xs) + 3 + len(pieces)),
        out_specs=[vmem()] * len(xs),
        compiler_params=pltpu.CompilerParams(vmem_limit_bytes=30 * MIB),
        cost_estimate=LIGHT,
        name="feed_forward",
    )(*xs, *own, *(piece for _, piece in pieces))


def add_kernel(*refs):
    refs[-1][...] = sum(ref[...].astype(F32) for ref in refs[:-1]).astype(BF16)


def add(parts):
    return pl.pallas_call(
        add_kernel,
        out_shape=jax.ShapeDtypeStruct(parts[0].shape, BF16),
        in_specs=[vmem()] * len(parts),
        out_specs=vmem(),
        compiler_params=pltpu.CompilerParams(vmem_limit_bytes=16 * MIB),
        cost_estimate=LIGHT,
        name="add_parts",
    )(*parts)


def next_kernel(whole, *refs):
    first_ref, wholes, halves = refs[0], refs[1 : 1 + whole], refs[1 + whole : -4]
    gain_ref, w_ref, sum_ref, out_ref = refs[-4:]
    extra = sum(ref[...].astype(F32) for ref in wholes)
    extra = extra + jnp.concatenate([ref[...].astype(F32) for ref in halves], axis=0)
    second = (first_ref[...].astype(F32) + extra).astype(BF16)
    sum_ref[...] = second
    normed = rms(second.astype(F32), gain_ref[...]).astype(BF16)
    out_ref[...] = dot(normed, w_ref[...]).astype(BF16)


def next_projection(first, wholes, halves, gains, w):
    rows, deep = first.shape
    width = w.shape[1]
    return pl.pallas_call(
        functools.partial(next_kernel, len(wholes)),
        out_shape=[
            jax.ShapeDtypeStruct((rows, deep), BF16),
            jax.ShapeDtypeStruct((rows, width), BF16),
        ],
        in_specs=[vmem()] * (3 + len(wholes) + len(halves)),
        out_specs=[vmem()] * 2,
        compiler_params=pltpu.CompilerParams(vmem_limit_bytes=40 * MIB),
        cost_estimate=LIGHT,
        name="next_projection",
    )(first, *wholes, *halves, gains, w)


def share_of(units, sharers):
    tall = -(-units // (16 * sharers)) * 16
    if tall < 64:
        return tall, [tall]
    front = -(-tall * FRONT // 1600) * 16
    return tall, [front, tall - front]


def first_unit(sharer, tall, units):
    return jnp.minimum(sharer * tall, units - tall)


def portion_kernel(gate, up, down, *refs):
    outs, (held, sems, out_sems) = refs[:-3], refs[-3:]
    tall = held.shape[1]
    at = first_unit(lax.axis_index("req"), tall, gate.shape[0])
    rows = pl.ds(pl.multiple_of(at, 16), tall)
    loads = [
        pltpu.make_async_copy(ref.at[rows], held.at[i], sems.at[i])
        for i, ref in enumerate((gate, up, down))
    ]
    for load in loads:
        load.start()
    for load in loads:
        load.wait()
    stores, at = [], 0
    for i, out in enumerate(outs):
        size = out.shape[1]
        stores.append(pltpu.make_async_copy(held.at[:, pl.ds(at, size)], out, out_sems.at[i]))
        stores[-1].start()
        at += size
    for store in stores:
        store.wait()


def portion(weights, sharers):
    units, deep = weights[0].shape
    tall, sizes = share_of(units, sharers)
    return pl.pallas_call(
        portion_kernel,
        out_shape=[jax.ShapeDtypeStruct((3, size, deep), BF16) for size in sizes],
        in_specs=[hbm()] * 3,
        out_specs=[hbm()] * len(sizes),
        scratch_shapes=[
            VMEM((3, tall, deep), BF16),
            pltpu.SemaphoreType.DMA((3,)),
            pltpu.SemaphoreType.DMA((len(sizes),)),
        ],
        compiler_params=pltpu.CompilerParams(vmem_limit_bytes=16 * MIB),
        cost_estimate=LIGHT,
        name="weight_share",
    )(*(stay(w) for w in weights))


def from_pair(part, width):
    return [lax.ppermute(part, "mlp", [(i, i ^ width) for i in range(DEPTH * width)])]


def swapped(part, bit):
    return lax.ppermute(part, "req", [(i, i ^ bit) for i in range(lax.axis_size("req"))])


def by_xor(blocks, axis):
    count = lax.axis_size(axis)
    return [blocks[0]] + [
        lax.ppermute(blocks[turn], axis, [(i, i ^ turn) for i in range(count)])
        for turn in range(1, count)
    ]


def after(values, *earlier):
    values, _ = lax.optimization_barrier((values, earlier))
    return values


def cached_state(prefix_state, prefix_norm, fd):
    heads, feats, hd = prefix_state.shape[1:]
    both = jnp.concatenate([prefix_state[0], prefix_norm[0][:, :, None]], axis=2).astype(BF16)
    ordered = jnp.concatenate([both[:, 1 + fd :], both[:, 1 : 1 + fd], both[:, :1]], axis=1)
    packed = jnp.pad(ordered, ((0, 0), (0, 15), (0, 128 - hd - 1)))
    return packed


def shards(
    residual_in,
    query_in,
    key_in,
    values_in,
    conv_weight,
    prefix_state,
    prefix_norm,
    prefix_owner,
    lengths,
    old_flags,
    out_weight,
    mlp_gain,
    gate_weight,
    up_weight,
    down_weight,
    next_gain,
    qkv_weight,
):
    mlp_count = lax.axis_size("mlp")
    width = mlp_count // DEPTH
    heads = prefix_state.shape[1]
    hd = values_in.shape[1] // (heads * mlp_count)
    fd = query_in.shape[1] // (heads * mlp_count)
    own = [gate_weight.T, up_weight.T, down_weight]

    sharers = lax.axis_size("req")
    packed = cached_state(prefix_state, prefix_norm, fd)
    states = list(enumerate(by_xor([packed] * sharers, "req")))
    tokens = pack(*(query_in, key_in, values_in), mlp_count)
    by_head = lax.all_to_all(tokens, "mlp", 0, 0, tiled=True)
    share = portion(after(own, tokens), sharers)
    count = len(share)
    lines = [from_pair(share[0], width)]
    by_head = after(by_head, share)
    attended = attention(
        lengths, old_flags, prefix_owner, by_head, conv_weight, states, heads, fd, hd
    )
    by_row = lax.all_to_all(attended, "mlp", 0, 0, tiled=True)
    by_row = by_row.reshape(mlp_count * heads * hd, by_row.shape[2])

    bits = [1 << i for i in reversed(range(sharers.bit_length() - 1))]

    def pass_on(held, bit):
        return held + [((part, flip ^ bit), swapped(piece, bit)) for (part, flip), piece in held]

    held = [((0, 0), piece) for piece in after(lines[0], attended)]
    for bit in bits[:-1]:
        held = pass_on(held, bit)
    for part in range(1, count):
        lines.append(from_pair(after(share[part], lines[-1], attended), width))
    first_sum, normed, parts = project(after(by_row, lines[0]), out_weight, residual_in, mlp_gain[None])

    def across(data):
        return lax.ppermute(data, "mlp", [(i, (i + mlp_count // 2) % mlp_count) for i in range(mlp_count)])

    def beside(data, turn):
        return lax.ppermute(
            data, "mlp", [(i, i - i % width + (i + turn) % width) for i in range(mlp_count)]
        )

    turns = range(1, width)
    near = [beside(normed, turn) for turn in turns]
    far = [across(parts[0])]
    arrived, near = after(([piece for _, piece in held], near), far[0])
    held = list(zip([key for key, _ in held], arrived))
    for part, piece in enumerate(lines[1:], 1):
        rest = [((part, 0), one) for one in piece]
        for bit in bits[:-1]:
            rest = pass_on(rest, bit)
        held = held + rest
    far_near = []
    for part in parts[1:]:
        sent = after(far[-1], near, *far_near)
        far.append(across(after(part, near, far)))
        far_near.append([beside(sent, turn) for turn in turns])
    sent = after(far[-1], far_near)
    far_near.append([beside(sent, turn) for turn in turns])
    pieces = [(key, after(piece, far_near[0], far[-1])) for key, piece in held]
    pieces = pass_on(pieces, bits[-1])
    back, sums, fed = [], [], []
    for mine, others in zip(far, far_near):
        fed.append(mlp(after([mine, *others], fed), own, pieces))
    for kept, *sent in fed:
        sums.append(add([kept] + [beside(part, -turn) for turn, part in zip(turns, sent)]))
        back.append(across(after(sums[-1], back)))
    part_own, *part_near = mlp(after([normed, *near], sums[0]), own, pieces)
    near_back = [beside(part, -turn) for turn, part in zip(turns, part_near)]
    return next_projection(first_sum, [part_own, *near_back], back, next_gain[None], qkv_weight)


def solution(mesh):
    rows = P(("req", "mlp"), None)
    placed = (
        rows,
        rows,
        rows,
        rows,
        P(),
        P("req", "mlp", None, None),
        P("req", "mlp", None),
        P(),
        P("req", None),
        P("req", None),
        P(),
        P(),
        P(None, "mlp"),
        P(None, "mlp"),
        P("mlp", None),
        P(),
        P(),
    )
    return jax.shard_map(
        shards, mesh=mesh, in_specs=placed, out_specs=(rows, rows), check_vma=False
    )
```

```python
import functools
import math

import jax
import jax.numpy as jnp
from jax import lax
from jax.experimental import pallas as pl
from jax.experimental.pallas import tpu as pltpu
from jax.sharding import PartitionSpec as P

EPSILON = 1e-05
DEPTH = 4
TURNED = (((1,), (1,)), ((), ()))
MIB = 1 << 20
ACROSS = (((0,), (0,)), ((), ()))
PLAIN = (((1,), (0,)), ((), ()))
F32 = jnp.float32
BF16 = jnp.bfloat16
VMEM = pltpu.VMEM
GRANT = 60 * MIB
FRONT = (30, 40)
PARTS = 2
LIGHT = pl.CostEstimate(flops=1, bytes_accessed=1, transcendentals=0)


def vmem():
    return pl.BlockSpec(memory_space=VMEM)


def dot(a, b, dims=PLAIN):
    return lax.dot_general(a, b, dims, preferred_element_type=F32)


def hbm():
    return pl.BlockSpec(memory_space=pltpu.HBM)


def stay(x):
    return pltpu.with_memory_space_constraint(x, pltpu.HBM)


def pack_kernel(q_hbm, k_hbm, v_hbm, out_hbm, q, k, v, out, sems):
    count = out.shape[0]
    loads = [
        pltpu.make_async_copy(src, dst, sems.at[i])
        for i, (src, dst) in enumerate(((q_hbm, q), (k_hbm, k), (v_hbm, v)))
    ]
    for load in loads:
        load.start()
    at = 0
    for load, ref in zip(loads, (q, k, v)):
        load.wait()
        part = ref.shape[1] // count
        turned = ref[...].T
        for m in range(count):
            out[m, at : at + part, :] = turned[m * part : (m + 1) * part, :]
        at += part
    store = pltpu.make_async_copy(out, out_hbm, sems.at[3])
    store.start()
    store.wait()


def pack(q, k, v, count):
    rows = (q.shape[1] + k.shape[1] + v.shape[1]) // count
    shape = (count, rows, q.shape[0])
    return pl.pallas_call(
        pack_kernel,
        out_shape=jax.ShapeDtypeStruct(shape, BF16),
        in_specs=[hbm()] * 3,
        out_specs=hbm(),
        scratch_shapes=[
            VMEM(q.shape, BF16),
            VMEM(k.shape, BF16),
            VMEM(v.shape, BF16),
            VMEM(shape, BF16),
            pltpu.SemaphoreType.DMA((4,)),
        ],
        compiler_params=pltpu.CompilerParams(vmem_limit_bytes=24 * MIB),
        cost_estimate=LIGHT,
        name="pack_heads",
    )(stay(q), stay(k), stay(v))


def attention_kernel(heads, fd, hd, turns, *refs):
    lengths_ref, flags_ref, owner_ref, conv_ref = refs[:4]
    states, refs = refs[4 : 5 + len(turns)], refs[5 + len(turns) :]
    x_hbm, out_hbm, turned, vconv, feats, taps, cached, out_ref, in_sems, state_sem, out_sems = refs
    blocks, rows, local = x_hbm.shape
    tokens = blocks * local
    values_at = 2 * heads * fd
    tile = 256 if tokens % 256 == 0 else local
    me = lax.axis_index("mlp")
    loads = [
        pltpu.make_async_copy(x_hbm.at[m], turned.at[:, pl.ds(m * local, local)], in_sems.at[m])
        for m in range(blocks)
    ]
    for load in loads:
        load.start()
    slot = lax.axis_index("req")
    owner = owner_ref[slot]
    here = [(slot ^ turn) == owner for turn in turns]
    for chosen, state in zip(here + [((slot ^ owner) & 1) == 1], states):

        @pl.when(chosen)
        def _():
            pltpu.make_async_copy(state, cached, state_sem).start()

    position = lax.broadcasted_iota(jnp.int32, (1, tokens), 1)
    start = jnp.zeros((1, tokens), jnp.int32)
    flag = jnp.zeros((1, tokens), F32) + flags_ref[0, 0].astype(F32)
    boundary = jnp.int32(0)
    for r in range(1, lengths_ref.shape[1]):
        boundary = boundary + lengths_ref[0, r - 1]
        reached = position >= boundary
        start = jnp.where(reached, boundary, start)
        flag = jnp.where(reached, flags_ref[0, r].astype(F32), flag)

    count = conv_ref.shape[0]
    spare = jnp.zeros((8 - count, conv_ref.shape[1]), F32)
    taps[...] = jnp.concatenate([conv_ref[...], spare], axis=0).T
    mine = pl.multiple_of(me * heads * hd, 8)
    weights = taps[pl.ds(mine, heads * hd), :]
    for load in loads:
        load.wait()
    values = turned[values_at:, :].astype(F32)
    total = weights[:, 0:1] * values
    for tap in range(1, count):
        earlier = pltpu.roll(values, tap, 1)
        total = total + weights[:, tap : tap + 1] * jnp.where(position - tap >= start, earlier, 0.0)
    vconv[...] = total.astype(BF16)

    for h in range(heads):
        wide = turned[h * fd : (h + 1) * fd, :].astype(F32)
        scaled = wide * (1.0 / math.sqrt(2.0 * fd))
        for a in range(fd):
            feats[h, a * fd : (a + 1) * fd, :] = (wide[a : a + 1, :] * scaled).astype(BF16)
        feats[h, fd * fd : fd * fd + fd, :] = (wide * fd ** (-0.25)).astype(BF16)
        ones = lax.broadcasted_iota(jnp.int32, (16, tokens), 0) == 0
        feats[h, fd * fd + fd :, :] = ones.astype(F32).astype(BF16)
    pltpu.make_async_copy(states[0], cached, state_sem).wait()
    stores = []
    for first in range(0, tokens, tile):
        last = first + tile
        flags = flag[:, first:last]
        key_at = lax.broadcasted_iota(jnp.int32, (last, tile), 0)
        visible = (key_at >= start[:, first:last]) & (key_at <= position[:, first:last])
        for h in range(heads):
            key = turned[(heads + h) * fd : (heads + h + 1) * fd, :last]
            old = dot(cached[h], feats[h, :, first:last], ACROSS)
            score = dot(key, turned[h * fd : (h + 1) * fd, first:last], ACROSS) * (fd**-0.5) + 1.0
            score = jnp.where(visible, score * score * 0.5 + 0.5, 0.0)
            den = jnp.sum(score, axis=0, keepdims=True) + flags * old[hd : hd + 1, :]
            num = dot(vconv[h * hd : (h + 1) * hd, :last], score.astype(BF16))
            result = ((num + flags * old[:hd, :]) / den).astype(BF16)
            for at in range(first, last, local):
                out_ref[at // local, h * hd : (h + 1) * hd, :] = result[:, at - first : at - first + local]
        for m in range(first // local, last // local):
            stores.append(pltpu.make_async_copy(out_ref.at[m], out_hbm.at[m], out_sems.at[m]))
            stores[-1].start()
    for store in stores:
        store.wait()


def attention(lengths, flags, owner, x, conv, states, heads, fd, hd):
    blocks, rows, local = x.shape
    tokens = blocks * local
    turns = tuple(turn for turn, _ in states[:-1])
    arrays = [state for _, state in states]
    return pl.pallas_call(
        functools.partial(attention_kernel, heads, fd, hd, turns),
        out_shape=jax.ShapeDtypeStruct((blocks, heads * hd, local), BF16),
        in_specs=[pl.BlockSpec(memory_space=pltpu.SMEM)] * 3
        + [vmem()]
        + [hbm()] * (len(arrays) + 1),
        out_specs=hbm(),
        scratch_shapes=[
            VMEM((rows, tokens), BF16),
            VMEM((heads * hd, tokens), BF16),
            VMEM((heads, arrays[0].shape[1], tokens), BF16),
            VMEM((conv.shape[1], 8), F32),
            VMEM(arrays[0].shape, BF16),
            VMEM((blocks, heads * hd, local), BF16),
            pltpu.SemaphoreType.DMA((blocks,)),
            pltpu.SemaphoreType.DMA,
            pltpu.SemaphoreType.DMA((blocks,)),
        ],
        compiler_params=pltpu.CompilerParams(vmem_limit_bytes=GRANT),
        cost_estimate=LIGHT,
        name="attention",
    )(lengths, flags, owner, conv, *arrays, x)


def rms(rows, gain):
    return rows * lax.rsqrt(jnp.mean(rows * rows, axis=-1, keepdims=True) + EPSILON) * gain


def project_kernel(att_hbm, w_hbm, res_hbm, gain_ref, sum_ref, normed_ref, *refs):
    halves, (att, res, w, sems) = refs[:-4], refs[-4:]
    half = w.shape[0] // 2
    loads = [
        pltpu.make_async_copy(src, dst, sems.at[i])
        for i, (src, dst) in enumerate(
            (
                (att_hbm, att),
                (w_hbm.at[pl.ds(0, half)], w.at[pl.ds(0, half)]),
                (w_hbm.at[pl.ds(half, half)], w.at[pl.ds(half, half)]),
                (res_hbm, res),
            )
        )
    ]
    for load in loads:
        load.start()
    loads[0].wait()
    rows = att[...].T
    loads[1].wait()
    projected = dot(rows[:, :half], w[:half, :])
    loads[2].wait()
    projected = projected + dot(rows[:, half:], w[half:, :])
    loads[3].wait()
    summed = (res[...].astype(F32) + projected).astype(BF16)
    sum_ref[...] = summed
    normed = rms(summed.astype(F32), gain_ref[...]).astype(BF16)
    normed_ref[...] = normed
    step = halves[0].shape[0]
    for i, half in enumerate(halves):
        half[...] = normed[i * step : (i + 1) * step]


def project(att, w, residual, gains):
    rows = att.shape[1]
    width = w.shape[1]
    full = jax.ShapeDtypeStruct((rows, width), BF16)
    part = jax.ShapeDtypeStruct((rows // PARTS, width), BF16)
    first_sum, normed, *halves = pl.pallas_call(
        project_kernel,
        out_shape=[full] * 2 + [part] * PARTS,
        in_specs=[hbm()] * 3 + [vmem()],
        out_specs=[vmem()] * (2 + PARTS),
        scratch_shapes=[
            VMEM(att.shape, BF16),
            VMEM(residual.shape, BF16),
            VMEM(w.shape, BF16),
            pltpu.SemaphoreType.DMA((4,)),
        ],
        compiler_params=pltpu.CompilerParams(vmem_limit_bytes=40 * MIB),
        cost_estimate=LIGHT,
        name="out_projection",
    )(att, stay(w), stay(residual), gains)
    return first_sum, normed, halves


def mlp_kernel(inputs, flips, sharers, *refs):
    xs, own, refs = refs[:inputs], refs[inputs : inputs + 3], refs[inputs + 3 :]
    pieces, outs = refs[:-inputs], refs[-inputs:]
    x = xs[0][...] if inputs == 1 else jnp.concatenate([ref[...] for ref in xs], axis=0)
    units = own[0].shape[0]
    tall, sizes = share_of(units, sharers)
    column = lax.broadcasted_iota(jnp.int32, (1, sum(ref.shape[1] for ref in pieces)), 1)
    fresh, at = column * 0, 0
    for part, flip in flips:
        sharer = lax.axis_index("req") ^ flip
        repeated = sharer * tall - first_unit(sharer, tall, units) - sum(sizes[:part])
        fresh = jnp.where(column >= at, at + repeated, fresh)
        at += sizes[part]
    total = None
    for gates, ups, downs in ([[ref] for ref in own], [[ref.at[i] for ref in pieces] for i in range(3)]):
        gate, up = (
            dot(x, jnp.concatenate([ref[...] for ref in group], axis=0), TURNED)
            for group in (gates, ups)
        )
        hidden = gate * jax.nn.sigmoid(gate) * up
        if gates[0] is not own[0]:
            hidden = jnp.where(column >= fresh, hidden, 0.0)
        part = dot(hidden.astype(BF16), jnp.concatenate([ref[...] for ref in downs], axis=0))
        total = part if total is None else total + part
    local = xs[0].shape[0]
    for i, out in enumerate(outs):
        out[...] = total[i * local : (i + 1) * local].astype(BF16)


def mlp(xs, own, pieces):
    rows, deep = xs[0].shape
    flips = [flip for flip, _ in pieces]
    return pl.pallas_call(
        functools.partial(mlp_kernel, len(xs), flips, lax.axis_size("req")),
        out_shape=[jax.ShapeDtypeStruct((rows, deep), BF16)] * len(xs),
        in_specs=[vmem()] * (len(xs) + 3 + len(pieces)),
        out_specs=[vmem()] * len(xs),
        compiler_params=pltpu.CompilerParams(vmem_limit_bytes=30 * MIB),
        cost_estimate=LIGHT,
        name="feed_forward",
    )(*xs, *own, *(piece for _, piece in pieces))


def add_kernel(*refs):
    refs[-1][...] = sum(ref[...].astype(F32) for ref in refs[:-1]).astype(BF16)


def add(parts):
    return pl.pallas_call(
        add_kernel,
        out_shape=jax.ShapeDtypeStruct(parts[0].shape, BF16),
        in_specs=[vmem()] * len(parts),
        out_specs=vmem(),
        compiler_params=pltpu.CompilerParams(vmem_limit_bytes=16 * MIB),
        cost_estimate=LIGHT,
        name="add_parts",
    )(*parts)


def next_kernel(whole, *refs):
    first_ref, wholes, halves = refs[0], refs[1 : 1 + whole], refs[1 + whole : -4]
    gain_ref, w_ref, sum_ref, out_ref = refs[-4:]
    extra = sum(ref[...].astype(F32) for ref in wholes)
    extra = extra + jnp.concatenate([ref[...].astype(F32) for ref in halves], axis=0)
    second = (first_ref[...].astype(F32) + extra).astype(BF16)
    sum_ref[...] = second
    normed = rms(second.astype(F32), gain_ref[...]).astype(BF16)
    out_ref[...] = dot(normed, w_ref[...]).astype(BF16)


def next_projection(first, wholes, halves, gains, w):
    rows, deep = first.shape
    width = w.shape[1]
    return pl.pallas_call(
        functools.partial(next_kernel, len(wholes)),
        out_shape=[
            jax.ShapeDtypeStruct((rows, deep), BF16),
            jax.ShapeDtypeStruct((rows, width), BF16),
        ],
        in_specs=[vmem()] * (3 + len(wholes) + len(halves)),
        out_specs=[vmem()] * 2,
        compiler_params=pltpu.CompilerParams(vmem_limit_bytes=40 * MIB),
        cost_estimate=LIGHT,
        name="next_projection",
    )(first, *wholes, *halves, gains, w)


def share_of(units, sharers):
    tall = -(-units // (16 * sharers)) * 16
    if tall < 96:
        return tall, [tall]
    front, middle = (tall * part // 1600 * 16 for part in FRONT)
    return tall, [front, middle, tall - front - middle]


def first_unit(sharer, tall, units):
    return jnp.minimum(sharer * tall, units - tall)


def portion_kernel(gate, up, down, *refs):
    outs, (held, sems, out_sems) = refs[:-3], refs[-3:]
    tall = held.shape[1]
    at = first_unit(lax.axis_index("req"), tall, gate.shape[0])
    rows = pl.ds(pl.multiple_of(at, 16), tall)
    loads = [
        pltpu.make_async_copy(ref.at[rows], held.at[i], sems.at[i])
        for i, ref in enumerate((gate, up, down))
    ]
    for load in loads:
        load.start()
    for load in loads:
        load.wait()
    stores, at = [], 0
    for i, out in enumerate(outs):
        size = out.shape[1]
        stores.append(pltpu.make_async_copy(held.at[:, pl.ds(at, size)], out, out_sems.at[i]))
        stores[-1].start()
        at += size
    for store in stores:
        store.wait()


def portion(weights, sharers):
    units, deep = weights[0].shape
    tall, sizes = share_of(units, sharers)
    return pl.pallas_call(
        portion_kernel,
        out_shape=[jax.ShapeDtypeStruct((3, size, deep), BF16) for size in sizes],
        in_specs=[hbm()] * 3,
        out_specs=[hbm()] * len(sizes),
        scratch_shapes=[
            VMEM((3, tall, deep), BF16),
            pltpu.SemaphoreType.DMA((3,)),
            pltpu.SemaphoreType.DMA((len(sizes),)),
        ],
        compiler_params=pltpu.CompilerParams(vmem_limit_bytes=16 * MIB),
        cost_estimate=LIGHT,
        name="weight_share",
    )(*(stay(w) for w in weights))


def from_pair(part, width):
    return [lax.ppermute(part, "mlp", [(i, i ^ width) for i in range(DEPTH * width)])]


def swapped(part, bit):
    return lax.ppermute(part, "req", [(i, i ^ bit) for i in range(lax.axis_size("req"))])


def spread_state(packed, owners):
    slots = lax.axis_size("req")
    me = lax.axis_index("req")
    held = [(0, packed)]
    bit = slots // 2
    while bit > 1:
        held += [(turn ^ bit, swapped(state, bit)) for turn, state in held]
        bit //= 2
    wanted = owners[me ^ 1]
    chosen = packed
    for turn, state in held[1:]:
        chosen = jnp.where((me ^ turn) == wanted, state, chosen)
    return held + [(1, swapped(chosen, 1))]


def by_xor(blocks, axis):
    count = lax.axis_size(axis)
    return [blocks[0]] + [
        lax.ppermute(blocks[turn], axis, [(i, i ^ turn) for i in range(count)])
        for turn in range(1, count)
    ]


def after(values, *earlier):
    values, _ = lax.optimization_barrier((values, earlier))
    return values


def cached_state(prefix_state, prefix_norm, fd):
    heads, feats, hd = prefix_state.shape[1:]
    both = jnp.concatenate([prefix_state[0], prefix_norm[0][:, :, None]], axis=2).astype(BF16)
    ordered = jnp.concatenate([both[:, 1 + fd :], both[:, 1 : 1 + fd], both[:, :1]], axis=1)
    packed = jnp.pad(ordered, ((0, 0), (0, 15), (0, 128 - hd - 1)))
    return packed


def shards(
    residual_in,
    query_in,
    key_in,
    values_in,
    conv_weight,
    prefix_state,
    prefix_norm,
    prefix_owner,
    lengths,
    old_flags,
    out_weight,
    mlp_gain,
    gate_weight,
    up_weight,
    down_weight,
    next_gain,
    qkv_weight,
):
    mlp_count = lax.axis_size("mlp")
    width = mlp_count // DEPTH
    heads = prefix_state.shape[1]
    hd = values_in.shape[1] // (heads * mlp_count)
    fd = query_in.shape[1] // (heads * mlp_count)
    own = [gate_weight.T, up_weight.T, down_weight]

    sharers = lax.axis_size("req")
    packed = cached_state(prefix_state, prefix_norm, fd)
    states = spread_state(packed, prefix_owner)
    share = portion(own, sharers)
    count = len(share)
    tokens = pack(*after((query_in, key_in, values_in), share), mlp_count)
    by_head = lax.all_to_all(tokens, "mlp", 0, 0, tiled=True)

    bits = [1 << i for i in reversed(range(sharers.bit_length() - 1))]

    def pass_on(held, bit):
        return held + [((part, flip ^ bit), swapped(piece, bit)) for (part, flip), piece in held]

    def keep(held, *earlier):
        pieces = after([piece for _, piece in held], *earlier)
        return list(zip([key for key, _ in held], pieces))

    lines = [from_pair(share[0], width)]
    front = [((0, 0), piece) for piece in after(lines[0], [state for _, state in states[:-1]])]
    for bit in bits[:-1]:
        front = pass_on(front, bit)
    by_head = after(by_head, [piece for _, piece in front])
    for part in range(1, count - 1):
        lines.append(from_pair(after(share[part], lines[-1]), width))
    attended = attention(
        lengths, old_flags, prefix_owner, by_head, conv_weight, states, heads, fd, hd
    )
    by_row = lax.all_to_all(attended, "mlp", 0, 0, tiled=True)
    by_row = by_row.reshape(mlp_count * heads * hd, by_row.shape[2])

    held = [
        ((part, 0), piece) for part, line in enumerate(lines[1:], 1) for piece in after(line, attended)
    ]
    for bit in bits[:-1]:
        held = pass_on(held, bit)
    if count > 1:
        lines.append(from_pair(after(share[-1], lines[-1], attended), width))
    first_sum, normed, parts = project(after(by_row, lines[:-1]), out_weight, residual_in, mlp_gain[None])

    def across(data):
        return lax.ppermute(data, "mlp", [(i, (i + mlp_count // 2) % mlp_count) for i in range(mlp_count)])

    def beside(data, turn):
        return lax.ppermute(
            data, "mlp", [(i, i - i % width + (i + turn) % width) for i in range(mlp_count)]
        )

    turns = range(1, width)
    near = [beside(normed, turn) for turn in turns]
    far = [across(parts[0])]
    arrived, near = after(([piece for _, piece in held], near), far[0])
    held = list(zip([key for key, _ in held], arrived))
    front, held = front + held, []
    if count > 1:
        held = [((count - 1, 0), piece) for piece in lines[-1]]
        for bit in bits[:-1]:
            held = pass_on(held, bit)
    far_near = []
    for part in parts[1:]:
        sent = after(far[-1], near, *far_near)
        far.append(across(after(part, near, far)))
        far_near.append([beside(sent, turn) for turn in turns])
    sent = after(far[-1], far_near)
    far_near.append([beside(sent, turn) for turn in turns])
    front = pass_on(keep(front, far[0]), bits[-1])
    pieces = front + pass_on(keep(held, far_near[0], far[-1]), bits[-1])
    back, sums, fed = [], [], []
    for mine, others in zip(far, far_near):
        fed.append(mlp(after([mine, *others], fed), own, pieces))
    for kept, *sent in fed:
        sums.append(add([kept] + [beside(part, -turn) for turn, part in zip(turns, sent)]))
        back.append(across(after(sums[-1], back)))
    part_own, *part_near = mlp(after([normed, *near], sums[0]), own, pieces)
    near_back = [beside(part, -turn) for turn, part in zip(turns, part_near)]
    return next_projection(first_sum, [part_own, *near_back], back, next_gain[None], qkv_weight)


def solution(mesh):
    rows = P(("req", "mlp"), None)
    placed = (
        rows,
        rows,
        rows,
        rows,
        P(),
        P("req", "mlp", None, None),
        P("req", "mlp", None),
        P(),
        P("req", None),
        P("req", None),
        P(),
        P(),
        P(None, "mlp"),
        P(None, "mlp"),
        P("mlp", None),
        P(),
        P(),
    )
    return jax.shard_map(
        shards, mesh=mesh, in_specs=placed, out_specs=(rows, rows), check_vma=False
    )
```
